256 devices in a mesh: head: 2 (over y_lo), inner: 8 (over z), outer: 16 (over x, y_hi, core).
Axes of the slice: x: 4, y: 4 (y_hi: 2, y_lo: 2; y = y_hi * 2 + y_lo), z: 8, core: 2. Of those that a mesh axis runs over, the one named last changes fastest.
Arguments:
- queries: bfloat16 [16384, 512], P(('outer', 'inner', 'head')), may hold values from -8 to 8
- keys: bfloat16 [16384, 512], P(('outer', 'inner', 'head')), may hold values from -8 to 8
- values: bfloat16 [16384, 512], P(('outer', 'inner', 'head')), may hold values from -6 to 6
- grad_out: bfloat16 [16384, 512], P(('outer', 'inner', 'head')), may hold values from -6 to 6
- saved_out: bfloat16 [16384, 512], P(('outer', 'inner', 'head')), may hold values from -3 to 3
- segment_ids: int32 [16384], replicated, may hold values from 0 to 31, never falling along the last dimension, each value on 1 to 1024 neighbouring positions
Outputs:
- grad_queries: bfloat16 [16384, 512], P(('outer', 'inner', 'head'))
- grad_keys: bfloat16 [16384, 512], P(('outer', 'inner', 'head'))
- grad_values: bfloat16 [16384, 512], P(('outer', 'inner', 'head'))
The draws below stay inside these ranges and needn't reach their ends.
Inputs may be any that keep to these rules, and one draw needn't show every extreme that they name: `segment_ids`: recording numbers never fall along the frames; every recording holds 1 to 1024 frames and one holds exactly 1024.
All inputs are finite; a program needn't handle non-finite values.
Results may differ from the reference program's by a relative error of at most 0.005.
Values may be sent and summed in bfloat16 or wider, within the bound.
No kernel may reach another device: no remote copies, remote signals or barrier semaphores. Data moves between devices by JAX's collectives and lax.ppermute only.
A program may use at most 64 MiB of HBM per device.

```python
import math
import jax
import jax.numpy as jnp
import numpy as np
from jax import lax

HEADS = 8
HD = 64
BOARD = 1024
SEQ = 16384
SEGS = 32


def draw_queries(key, part):
    key = jax.random.fold_in(key, 11)
    drawn = jax.random.truncated_normal(key, -4.0, 4.0, (SEQ, HEADS * HD))
    return drawn.astype(jnp.bfloat16)


def draw_keys(key, part):
    key = jax.random.fold_in(key, 23)
    drawn = jax.random.truncated_normal(key, -4.0, 4.0, (SEQ, HEADS * HD))
    return drawn.astype(jnp.bfloat16)


def block_scale(own_key, extent, shards, low, top_value):
    level = 1.0
    for axis_at, blocks in shards:
        steps = jax.random.uniform(jax.random.fold_in(jax.random.fold_in(own_key, 6), axis_at), (blocks,), jnp.float32, low / len(shards), top_value / len(shards))
        level = level * jnp.repeat(jnp.exp(steps), extent[axis_at] // blocks).reshape((-1,) + (1,) * (len(extent) - 1 - axis_at))
    return level


def split_up(number_of, total, bound, lean):
    portions = [(1 << 20) // math.isqrt(rank ** lean) + 1 for rank in range(2, number_of + 1)]
    spare, given = total - bound - (number_of - 1), [1] * (number_of - 1)
    while spare > 0:
        free = [i for i in range(number_of - 1) if given[i] < bound]
        mass, budget = sum([portions[i] for i in free]), spare
        for i in free:
            addition = min(bound - given[i], max(1, budget * portions[i] // mass), spare)
            given[i] = given[i] + addition
            spare = spare - addition
    return np.array([bound] + given)


def ragged_sizes(own_key, count, total, limit, lean):
    if count == 2:
        one = jax.random.randint(own_key, (), max(1, total - limit), min(limit, total - 1) + 1)
        return jnp.stack([one, total - one])
    sizes = jnp.asarray(split_up(count, total, limit, lean), jnp.int32)
    twos = (count - 1) // 2
    giver, taker = sizes[1:1 + 2 * twos:2], sizes[2:2 + 2 * twos:2]
    slack = jnp.minimum(giver - 1, limit - taker)
    shifted = jax.random.randint(jax.random.fold_in(own_key, 1), (twos,), 0, 1 << 20) % (slack + 1)
    sizes = sizes.at[1:1 + 2 * twos:2].set(giver - shifted).at[2:2 + 2 * twos:2].set(taker + shifted)
    return sizes[jax.random.permutation(jax.random.fold_in(own_key, 2), count)]


def bell_draw(own_key, dims, spread, bound, cuts=(), kind=jnp.bfloat16):
    level = block_scale(own_key, dims, cuts, -0.22, 0.18) if cuts else 1.0
    values = jax.random.normal(own_key, dims, jnp.float32) * spread * level
    return jnp.minimum(jnp.maximum(values, -bound), bound).astype(kind)


def setup_inputs(seed: int = 0) -> dict:
    splits = jax.random.split(jax.random.key(seed), 7)
    queries = draw_queries(jax.random.fold_in(splits[6], 71), 0)
    keys = draw_keys(jax.random.fold_in(splits[6], 71), 0)
    values = bell_draw(splits[2], (SEQ, HEADS * HD), 1.0, 6.0, ((0, 256),))
    grad_out = bell_draw(splits[3], (SEQ, HEADS * HD), 1.0, 6.0, ((0, 256),))
    saved_out = bell_draw(splits[4], (SEQ, HEADS * HD), 0.5, 3.0, ((0, 256),))
    segment_ids = jnp.searchsorted(jnp.cumsum(ragged_sizes(splits[5], SEGS, SEQ, BOARD, 0)), jnp.arange(SEQ), side="right").astype(jnp.int32)
    return {"queries": queries, "keys": keys, "values": values, "grad_out": grad_out, "saved_out": saved_out, "segment_ids": segment_ids}


def reference(queries, keys, values, grad_out, saved_out, segment_ids):
    scaling = 1.0 / math.sqrt(HD)
    window = min(SEQ, 3 * BOARD)
    query_heads = queries.reshape(SEQ, HEADS, HD)
    key_heads = keys.reshape(SEQ, HEADS, HD)
    value_heads = values.reshape(SEQ, HEADS, HD)
    grad_heads = grad_out.reshape(SEQ, HEADS, HD)
    saved_heads = saved_out.reshape(SEQ, HEADS, HD)
    deltas = lax.optimization_barrier(jnp.sum(grad_heads.astype(jnp.float32) * saved_heads.astype(jnp.float32), axis=2))

    def block_step(totals, block_num):
        grad_keys, grad_values = totals
        begin_at = (block_num * BOARD).astype(jnp.int32)
        window_at = jnp.clip(begin_at - BOARD, 0, SEQ - window).astype(jnp.int32)
        query_block = lax.dynamic_slice_in_dim(query_heads, begin_at, BOARD, 0).astype(jnp.float32)
        grad_block = lax.dynamic_slice_in_dim(grad_heads, begin_at, BOARD, 0).astype(jnp.float32)
        delta_block = lax.dynamic_slice_in_dim(deltas, begin_at, BOARD, 0)
        query_labels = lax.dynamic_slice_in_dim(segment_ids, begin_at, BOARD, 0)
        key_window = lax.dynamic_slice_in_dim(key_heads, window_at, window, 0).astype(jnp.float32)
        value_window = lax.dynamic_slice_in_dim(value_heads, window_at, window, 0).astype(jnp.float32)
        key_labels = lax.dynamic_slice_in_dim(segment_ids, window_at, window, 0)
        allowed = (query_labels[:, None] == key_labels[None, :])[None]
        scores = scaling * jnp.einsum('qhd,khd->hqk', query_block, key_window)
        masked = jnp.where(allowed, scores, -jnp.inf)
        highest = lax.optimization_barrier(jnp.max(masked, axis=2, keepdims=True))
        log_totals = highest + jnp.log(lax.optimization_barrier(jnp.sum(jnp.exp(masked - highest), axis=2, keepdims=True)))
        weights = jnp.where(allowed, jnp.exp(scores - log_totals), 0.0)
        weights_low = lax.optimization_barrier(weights.astype(jnp.bfloat16)).astype(jnp.float32)
        grad_weights = jnp.einsum('qhd,khd->hqk', grad_block, value_window)
        grad_scores = weights * (grad_weights - jnp.transpose(delta_block)[:, :, None])
        scores_low = lax.optimization_barrier(grad_scores.astype(jnp.bfloat16)).astype(jnp.float32)
        grad_query = scaling * jnp.einsum('hqk,khd->qhd', scores_low, key_window)
        key_part = scaling * jnp.einsum('hqk,qhd->khd', scores_low, query_block)
        value_part = jnp.einsum('hqk,qhd->khd', weights_low, grad_block)
        grad_keys = lax.dynamic_update_slice_in_dim(grad_keys, lax.dynamic_slice_in_dim(grad_keys, window_at, window, 0) + key_part, window_at, 0)
        grad_values = lax.dynamic_update_slice_in_dim(grad_values, lax.dynamic_slice_in_dim(grad_values, window_at, window, 0) + value_part, window_at, 0)
        return ((grad_keys, grad_values), grad_query)
    zero_grads = jnp.zeros((SEQ, HEADS, HD), jnp.float32)
    (grad_keys, grad_values), grad_queries = lax.scan(block_step, (zero_grads, zero_grads), jnp.arange(SEQ // BOARD, dtype=jnp.int32))
    grad_queries = grad_queries.reshape(SEQ, HEADS * HD).astype(jnp.bfloat16)
    return (grad_queries, grad_keys.reshape(SEQ, HEADS * HD).astype(jnp.bfloat16), grad_values.reshape(SEQ, HEADS * HD).astype(jnp.bfloat16))
```

```python
import math

import jax
import jax.numpy as jnp
from jax import lax
from jax.experimental import pallas as pl
from jax.experimental.pallas import tpu as pltpu
from jax.sharding import PartitionSpec as P

HD = 64
ROWS = 64
LANES = 128
BLOCKS = 8
MSG = 2 * ROWS + 16
OUT_ROWS = ROWS + ROWS // 2
BOARD = 1024
GROUP = 128
BOARD_GROUPS = BOARD // GROUP
WINDOW = 3 * BOARD
GROUPS = WINDOW // GROUP
OWN = BLOCKS * ROWS
QT = 256
KC = 256
TILE = 256
PAD = KC
FAR = 2.0**100
NO_LABEL = 63
BITS = 6
LOWEST = -3e38
F32 = jnp.float32
BF16 = jnp.bfloat16


def rows_by_rows(left, right):
    return lax.dot_general(left, right, (((1,), (1,)), ((), ())), preferred_element_type=F32)


def rows_by_cols(left, right):
    return lax.dot_general(left, right, (((1,), (0,)), ((), ())), preferred_element_type=F32)


def half_turn(x):
    return pltpu.roll(x, HD, axis=1)


def low_lanes(rows):
    return lax.broadcasted_iota(jnp.int32, (rows, LANES), 1) < HD


def pack_kernel(q_ref, k_ref, v_ref, g_ref, s_ref, out_ref):
    low = low_lanes(ROWS)
    for pair in range(4):
        cols = slice(pair * LANES, (pair + 1) * LANES)
        q, k, v, g = (r[:, cols].astype(F32) for r in (q_ref, k_ref, v_ref, g_ref))
        out_ref[2 * pair, :ROWS] = jnp.where(low, q, half_turn(v)).astype(BF16)
        out_ref[2 * pair + 1, :ROWS] = jnp.where(low, half_turn(q), v).astype(BF16)
        out_ref[2 * pair, ROWS : 2 * ROWS] = jnp.where(low, k, half_turn(g)).astype(BF16)
        out_ref[2 * pair + 1, ROWS : 2 * ROWS] = jnp.where(low, half_turn(k), g).astype(BF16)
    cols = 8 * HD
    products = g_ref[...].astype(F32) * s_ref[...].astype(F32)
    high = products.astype(BF16)
    rest = (products - high.astype(F32)).astype(BF16)
    head_of = lax.broadcasted_iota(jnp.int32, (16, cols), 1) // HD
    wanted = lax.broadcasted_iota(jnp.int32, (16, cols), 0) % 8
    pick = jnp.where(head_of == wanted, 1.0, 0.0).astype(BF16)
    twice = lambda x: jnp.concatenate([x, x], axis=0)
    deltas = rows_by_rows(pick, twice(high)) + rows_by_rows(pick, twice(rest))
    first = deltas.astype(BF16).astype(F32)
    second = (deltas - first).astype(BF16).astype(F32)
    third = deltas - first - second
    row = lax.broadcasted_iota(jnp.int32, (16, LANES), 0)
    lowest = low_lanes(16)
    table = jnp.where(
        row < 8, jnp.where(lowest, first, second), jnp.where(lowest, third, 0.0)
    ).astype(BF16)
    for head in range(8):
        out_ref[head, 2 * ROWS :] = table


def pack(queries, keys, values, grad_out, saved_out):
    return pl.pallas_call(
        pack_kernel,
        out_shape=jax.ShapeDtypeStruct((8, MSG, LANES), BF16),
    )(queries, keys, values, grad_out, saved_out)


def unpack_kernel(in_ref, dq_ref, dk_ref, dv_ref):
    low = low_lanes(ROWS)
    low_half = low_lanes(ROWS // 2)
    for pair in range(4):
        cols = slice(pair * LANES, (pair + 1) * LANES)
        a = in_ref[2 * pair, :ROWS].astype(F32)
        b = in_ref[2 * pair + 1, :ROWS].astype(F32)
        dk_ref[:, cols] = jnp.where(low, a, half_turn(b)).astype(BF16)
        dv_ref[:, cols] = jnp.where(low, half_turn(a), b).astype(BF16)
        c = in_ref[2 * pair, ROWS:].astype(F32)
        d = in_ref[2 * pair + 1, ROWS:].astype(F32)
        dq_ref[: ROWS // 2, cols] = jnp.where(low_half, c, half_turn(d)).astype(BF16)
        dq_ref[ROWS // 2 :, cols] = jnp.where(low_half, half_turn(c), d).astype(BF16)


def unpack(results):
    shape = jax.ShapeDtypeStruct((ROWS, 8 * HD), BF16)
    return pl.pallas_call(unpack_kernel, out_shape=(shape, shape, shape))(results)


def features(ids, lane, lead):
    at = lane - lead
    second = at >= BITS
    bit = lax.shift_right_logical(ids, jnp.where(second, at - BITS, at) & 31) & 1
    used = jnp.logical_and(at >= 0, at < 2 * BITS)
    return used, jnp.where(second, 1 - bit, bit).astype(F32)


def main_kernel(
    meta, starts, ends, ids_ref, p0, p1, p2, p3, p4, p5, out_ref,
    xs, ys, qa, ka, xv, own_qa, own_ka, own_xv, own_y, lse, delta, acc,
):
    outer, head, parity = meta[0], meta[1], meta[2]
    base = (outer - 1) * BOARD
    lane = lax.broadcasted_iota(jnp.int32, (GROUP, LANES), 1)
    low = lane < HD
    low_row = low_lanes(1)
    sub16 = lax.broadcasted_iota(jnp.int32, (16, LANES), 0)
    delta_rows = jnp.logical_or(sub16 == head, sub16 == head + 8)

    pieces = ((p2, p3), (p0, p1), (p4, p5))
    swap = parity == 1
    for board in range(3):
        mine, other = pieces[board]
        for block in range(BLOCKS):
            group = board * BLOCKS + block
            for piece, side in ((mine, parity), (other, 1 - parity)):
                at = pl.multiple_of(group * GROUP + side * ROWS, ROWS)
                xs[pl.ds(at, ROWS), :] = piece[block, :ROWS]
                ys[pl.ds(at, ROWS), :] = piece[block, ROWS : 2 * ROWS]
            parts = []
            for piece in (mine, other):
                table = jnp.where(delta_rows, piece[block, 2 * ROWS :].astype(F32), 0.0)
                line = jnp.sum(table, axis=0, keepdims=True)
                parts.append(line + half_turn(line))
            delta[pl.ds(group, 1), :] = jnp.where(
                jnp.logical_xor(low_row, swap), parts[0], parts[1]
            )

    def prepare(group, carry):
        at = pl.multiple_of(group * GROUP, GROUP)
        board = outer - 1 + group // BOARD_GROUPS
        real = jnp.logical_and(board >= 0, board < ids_ref.shape[0] // BOARD_GROUPS)
        line = ids_ref[pl.ds(jnp.clip(base // GROUP + group, 0, ids_ref.shape[0] - 1), 1), :]
        line = jnp.where(real, line, NO_LABEL)
        ids = jnp.transpose(jnp.broadcast_to(line, (GROUP, LANES)))
        used, bits = features(ids, lane, HD)
        x = xs[pl.ds(at, GROUP), :].astype(F32)
        y = ys[pl.ds(at, GROUP), :].astype(F32)
        q_side = jnp.where(used, -FAR * bits, 0.0)
        k_side = jnp.where(used, 1.0 - bits, 0.0)
        qa[pl.ds(at, GROUP), :] = jnp.where(low, x * (1.0 / math.sqrt(HD)), q_side).astype(BF16)
        ka[pl.ds(at, GROUP), :] = jnp.where(low, y, k_side).astype(BF16)
        xv[pl.ds(at, GROUP), :] = jnp.where(low, 0.0, x).astype(BF16)
        return carry

    lax.fori_loop(0, GROUPS, prepare, 0)
    _, bits = features(jnp.full((PAD, LANES), NO_LABEL, jnp.int32),
                       lax.broadcasted_iota(jnp.int32, (PAD, LANES), 1), HD)
    pad_lane = lax.broadcasted_iota(jnp.int32, (PAD, LANES), 1)
    pad_used = jnp.logical_and(pad_lane >= HD, pad_lane < HD + 2 * BITS)
    zero = jnp.zeros((PAD, LANES), BF16)
    qa[WINDOW:, :] = jnp.where(pad_used, -FAR * bits, 0.0).astype(BF16)
    ka[WINDOW:, :] = jnp.where(pad_used, 1.0 - bits, 0.0).astype(BF16)
    xv[WINDOW:, :] = zero
    xs[WINDOW:, :] = zero
    ys[WINDOW:, :] = zero
    lse[...] = jnp.zeros_like(lse)
    delta[pl.ds(GROUPS, delta.shape[0] - GROUPS), :] = jnp.zeros(
        (delta.shape[0] - GROUPS, LANES), F32
    )

    for block in range(BLOCKS):
        at = pl.multiple_of(BOARD + block * GROUP + parity * ROWS, ROWS)
        to = pl.ds(block * ROWS, ROWS)
        own_qa[to, :] = qa[pl.ds(at, ROWS), :]
        own_ka[to, :] = ka[pl.ds(at, ROWS), :]
        own_xv[to, :] = xv[pl.ds(at, ROWS), :]
        own_y[to, :] = ys[pl.ds(at, ROWS), :]

    first = starts[outer * BOARD_GROUPS] - base
    last = ends[outer * BOARD_GROUPS + BOARD_GROUPS - 1] - base
    tile_groups = QT // GROUP

    def chunks(lo, hi):
        begin = lo // GROUP * GROUP
        return begin, (hi - begin + KC - 1) // KC

    def totals(tile, carry):
        at = pl.multiple_of(tile * QT, QT)
        group = outer * BOARD_GROUPS - BOARD_GROUPS + tile * tile_groups
        group_top = starts.shape[0] - 1
        lo = jnp.maximum(starts[jnp.clip(group, 0, group_top)] - base, first)
        hi = jnp.minimum(ends[jnp.clip(group + tile_groups - 1, 0, group_top)] - base, last)
        begin, count = chunks(lo, hi)
        queries = qa[pl.ds(at, QT), :]

        def step(num, state):
            top, total = state
            here = pl.multiple_of(begin + num * KC, GROUP)
            scores = rows_by_rows(ka[pl.ds(here, KC), :], queries).reshape(KC // 8, 8, QT)
            new_top = jnp.maximum(top, jnp.max(scores, axis=0))
            terms = jnp.sum(jnp.exp(scores - new_top[None]), axis=0)
            return new_top, total * jnp.exp(top - new_top) + terms

        top, total = lax.fori_loop(
            0, count, step, (jnp.full((8, QT), LOWEST, F32), jnp.zeros((8, QT), F32))
        )
        highest = jnp.max(top, axis=0, keepdims=True)
        line = highest + jnp.log(jnp.sum(total * jnp.exp(top - highest), axis=0, keepdims=True))
        line = jnp.where(highest < -0.5 * FAR, 0.0, line)
        for part in range(tile_groups):
            lse[pl.ds(tile * tile_groups + part, 1), :] = line[:, part * LANES : (part + 1) * LANES]
        return carry

    lax.fori_loop(first // QT, (last + QT - 1) // QT, totals, 0)

    tile_blocks = TILE // ROWS

    def own_columns(source, tile):
        columns = []
        for pair in range(tile_blocks // 2):
            group = BOARD_GROUPS + tile * tile_blocks + 2 * pair
            a, b = source[pl.ds(group, 1), :], source[pl.ds(group + 1, 1), :]
            line = jnp.where(
                low_row, jnp.where(swap, half_turn(a), a), jnp.where(swap, b, half_turn(b))
            )
            columns.append(jnp.transpose(jnp.broadcast_to(line, (GROUP, LANES))))
        return jnp.concatenate(columns, axis=0)

    def own_range(tile):
        group = outer * BOARD_GROUPS + tile * tile_blocks
        return chunks(starts[group] - base, ends[group + tile_blocks - 1] - base)

    for tile in range(OWN // TILE):
        rows = slice(tile * TILE, (tile + 1) * TILE)
        begin, count = own_range(tile)

        logs = jnp.concatenate([own_columns(lse, tile)] * (KC // LANES), axis=1)
        drops = jnp.concatenate([own_columns(delta, tile)] * (KC // LANES), axis=1)
        acc[...] = jnp.zeros_like(acc)

        def query_step(num, carry):
            here = pl.ds(pl.multiple_of(begin + num * KC, GROUP), KC)
            weights = jnp.exp(rows_by_rows(own_qa[rows, :], ka[here, :]) - logs)
            grads = weights * (rows_by_rows(own_y[rows, :], xv[here, :]) - drops)
            acc[0] += rows_by_cols(grads.astype(BF16), ys[here, :])
            return carry

        lax.fori_loop(0, count, query_step, 0)
        dq = acc[0] * (1.0 / math.sqrt(HD))
        low_half = low_lanes(ROWS // 2)
        for block in range(tile_blocks):
            upper = dq[block * ROWS : block * ROWS + ROWS // 2]
            lower = dq[block * ROWS + ROWS // 2 : (block + 1) * ROWS]
            out_ref[tile * tile_blocks + block, ROWS:] = jnp.where(
                low_half, upper, half_turn(lower)
            ).astype(BF16)

        acc[...] = jnp.zeros_like(acc)

        def key_step(num, carry):
            at = pl.multiple_of(begin + num * KC, GROUP)
            here = pl.ds(at, KC)
            lines = [(begin + num * KC) // GROUP + part for part in range(KC // LANES)]
            logs_row = jnp.concatenate([lse[pl.ds(n, 1), :] for n in lines], axis=1)
            drops_row = jnp.concatenate([delta[pl.ds(n, 1), :] for n in lines], axis=1)
            weights = jnp.exp(rows_by_rows(own_ka[rows, :], qa[here, :]) - logs_row)
            grads = weights * (rows_by_rows(own_xv[rows, :], ys[here, :]) - drops_row)
            acc[0] += rows_by_cols(grads.astype(BF16), xs[here, :])
            acc[1] += rows_by_cols(weights.astype(BF16), ys[here, :])
            return carry

        lax.fori_loop(0, count, key_step, 0)
        both = jnp.where(
            low_lanes(TILE), acc[0] * (1.0 / math.sqrt(HD)), acc[1]
        ).astype(BF16)
        for block in range(tile_blocks):
            out_ref[tile * tile_blocks + block, :ROWS] = both[block * ROWS : (block + 1) * ROWS]


def main(meta, starts, ends, ids, pieces):
    smem = pl.BlockSpec(memory_space=pltpu.SMEM)
    vmem = pl.BlockSpec(memory_space=pltpu.VMEM)
    window = pltpu.VMEM((WINDOW + PAD, LANES), BF16)
    own = pltpu.VMEM((OWN, LANES), BF16)
    lines = pltpu.VMEM((GROUPS + 8, LANES), F32)
    return pl.pallas_call(
        main_kernel,
        out_shape=jax.ShapeDtypeStruct((BLOCKS, OUT_ROWS, LANES), BF16),
        in_specs=[smem, smem, smem, vmem] + [vmem] * 6,
        out_specs=vmem,
        scratch_shapes=[window] * 5 + [own] * 4 + [lines] * 2
        + [pltpu.VMEM((2, TILE, LANES), F32)],
        compiler_params=pltpu.CompilerParams(vmem_limit_bytes=32 * 1024 * 1024),
    )(meta, starts, ends, ids, *pieces)


def moved(x, boards, flip):
    heads, outers = lax.axis_size("head"), lax.axis_size("outer")
    pairs = [
        (h * outers + i, (h ^ flip) * outers + i + boards)
        for h in range(heads)
        for i in range(outers)
        if 0 <= i + boards < outers
    ]
    return lax.ppermute(x, ("head", "outer"), pairs)


def local(queries, keys, values, grad_out, saved_out, segment_ids):
    ids = segment_ids.reshape(-1, GROUP)
    starts = jnp.sum(segment_ids[None, :] < ids[:, :1], axis=1, dtype=jnp.int32)
    ends = jnp.sum(segment_ids[None, :] <= ids[:, -1:], axis=1, dtype=jnp.int32)
    meta = jnp.stack([lax.axis_index("outer"), lax.axis_index("inner"), lax.axis_index("head")])
    message = pack(queries, keys, values, grad_out, saved_out)
    mine = lax.all_to_all(message, "inner", split_axis=0, concat_axis=0, tiled=True)
    pieces = (
        mine,
        moved(mine, 0, 1),
        moved(mine, 1, 0),
        moved(mine, 1, 1),
        moved(mine, -1, 0),
        moved(mine, -1, 1),
    )
    results = main(meta, starts, ends, ids, pieces)
    gathered = lax.all_to_all(results, "inner", split_axis=0, concat_axis=0, tiled=True)
    return unpack(gathered)


def solution(mesh):
    rows = P(("outer", "inner", "head"), None)
    return jax.shard_map(
        local,
        mesh=mesh,
        in_specs=(rows, rows, rows, rows, rows, P()),
        out_specs=(rows, rows, rows),
        check_vma=False,
    )
```

```python
import math

import jax
import jax.numpy as jnp
from jax import lax
from jax.experimental import pallas as pl
from jax.experimental.pallas import tpu as pltpu
from jax.sharding import PartitionSpec as P

HD = 64
ROWS = 64
LANES = 128
BLOCKS = 8
MSG = 2 * ROWS + 16
OUT_ROWS = ROWS + ROWS // 2
BOARD = 1024
GROUP = 128
BOARD_GROUPS = BOARD // GROUP
WINDOW = 3 * BOARD
GROUPS = WINDOW // GROUP
OWN = BLOCKS * ROWS
QT = 512
KT = 512
KC = 768
TILE = 256
PAD = max(KC, KT)
FAR = 2.0**100
NO_LABEL = 63
BITS = 6
LOWEST = -3e38
F32 = jnp.float32
BF16 = jnp.bfloat16


def rows_by_rows(left, right):
    return lax.dot_general(left, right, (((1,), (1,)), ((), ())), preferred_element_type=F32)


def rows_by_cols(left, right):
    return lax.dot_general(left, right, (((1,), (0,)), ((), ())), preferred_element_type=F32)


def half_turn(x):
    return pltpu.roll(x, HD, axis=1)


def low_lanes(rows):
    return lax.broadcasted_iota(jnp.int32, (rows, LANES), 1) < HD


def pack_kernel(q_ref, k_ref, v_ref, g_ref, s_ref, out_ref):
    low = low_lanes(ROWS)
    for pair in range(4):
        cols = slice(pair * LANES, (pair + 1) * LANES)
        q, k, v, g = (r[:, cols].astype(F32) for r in (q_ref, k_ref, v_ref, g_ref))
        out_ref[2 * pair, :ROWS] = jnp.where(low, q, half_turn(v)).astype(BF16)
        out_ref[2 * pair + 1, :ROWS] = jnp.where(low, half_turn(q), v).astype(BF16)
        out_ref[2 * pair, ROWS : 2 * ROWS] = jnp.where(low, k, half_turn(g)).astype(BF16)
        out_ref[2 * pair + 1, ROWS : 2 * ROWS] = jnp.where(low, half_turn(k), g).astype(BF16)
    cols = 8 * HD
    products = g_ref[...].astype(F32) * s_ref[...].astype(F32)
    high = products.astype(BF16)
    rest = (products - high.astype(F32)).astype(BF16)
    head_of = lax.broadcasted_iota(jnp.int32, (16, cols), 1) // HD
    wanted = lax.broadcasted_iota(jnp.int32, (16, cols), 0) % 8
    pick = jnp.where(head_of == wanted, 1.0, 0.0).astype(BF16)
    twice = lambda x: jnp.concatenate([x, x], axis=0)
    deltas = rows_by_rows(pick, twice(high)) + rows_by_rows(pick, twice(rest))
    first = deltas.astype(BF16).astype(F32)
    second = (deltas - first).astype(BF16).astype(F32)
    third = deltas - first - second
    row = lax.broadcasted_iota(jnp.int32, (16, LANES), 0)
    lowest = low_lanes(16)
    table = jnp.where(
        row < 8, jnp.where(lowest, first, second), jnp.where(lowest, third, 0.0)
    ).astype(BF16)
    for head in range(8):
        out_ref[head, 2 * ROWS :] = table


def pack(queries, keys, values, grad_out, saved_out):
    return pl.pallas_call(
        pack_kernel,
        out_shape=jax.ShapeDtypeStruct((8, MSG, LANES), BF16),
    )(queries, keys, values, grad_out, saved_out)


def unpack_kernel(in_ref, dq_ref, dk_ref, dv_ref):
    low = low_lanes(ROWS)
    low_half = low_lanes(ROWS // 2)
    for pair in range(4):
        cols = slice(pair * LANES, (pair + 1) * LANES)
        a = in_ref[2 * pair, :ROWS].astype(F32)
        b = in_ref[2 * pair + 1, :ROWS].astype(F32)
        dk_ref[:, cols] = jnp.where(low, a, half_turn(b)).astype(BF16)
        dv_ref[:, cols] = jnp.where(low, half_turn(a), b).astype(BF16)
        c = in_ref[2 * pair, ROWS:].astype(F32)
        d = in_ref[2 * pair + 1, ROWS:].astype(F32)
        dq_ref[: ROWS // 2, cols] = jnp.where(low_half, c, half_turn(d)).astype(BF16)
        dq_ref[ROWS // 2 :, cols] = jnp.where(low_half, half_turn(c), d).astype(BF16)


def unpack(results):
    shape = jax.ShapeDtypeStruct((ROWS, 8 * HD), BF16)
    return pl.pallas_call(unpack_kernel, out_shape=(shape, shape, shape))(results)


def features(ids, lane, lead):
    at = lane - lead
    second = at >= BITS
    bit = lax.shift_right_logical(ids, jnp.where(second, at - BITS, at) & 31) & 1
    used = jnp.logical_and(at >= 0, at < 2 * BITS)
    return used, jnp.where(second, 1 - bit, bit).astype(F32)


def main_kernel(
    meta, starts, ends, ids_ref, p0, p1, p2, p3, p4, p5, out_ref,
    xs, ys, qa, ka, xv, own_qa, own_ka, own_xv, own_y, lse, delta, acc,
):
    outer, head, parity = meta[0], meta[1], meta[2]
    base = (outer - 1) * BOARD
    lane = lax.broadcasted_iota(jnp.int32, (GROUP, LANES), 1)
    low = lane < HD
    low_row = low_lanes(1)
    sub16 = lax.broadcasted_iota(jnp.int32, (16, LANES), 0)
    delta_rows = jnp.logical_or(sub16 == head, sub16 == head + 8)

    pieces = ((p2, p3), (p0, p1), (p4, p5))
    swap = parity == 1
    for board in range(3):
        mine, other = pieces[board]
        for block in range(BLOCKS):
            group = board * BLOCKS + block
            for piece, side in ((mine, parity), (other, 1 - parity)):
                at = pl.multiple_of(group * GROUP + side * ROWS, ROWS)
                xs[pl.ds(at, ROWS), :] = piece[block, :ROWS]
                ys[pl.ds(at, ROWS), :] = piece[block, ROWS : 2 * ROWS]
            parts = []
            for piece in (mine, other):
                table = jnp.where(delta_rows, piece[block, 2 * ROWS :].astype(F32), 0.0)
                line = jnp.sum(table, axis=0, keepdims=True)
                parts.append(line + half_turn(line))
            delta[pl.ds(group, 1), :] = jnp.where(
                jnp.logical_xor(low_row, swap), parts[0], parts[1]
            )

    def prepare(group, carry):
        at = pl.multiple_of(group * GROUP, GROUP)
        board = outer - 1 + group // BOARD_GROUPS
        real = jnp.logical_and(board >= 0, board < ids_ref.shape[0] // BOARD_GROUPS)
        line = ids_ref[pl.ds(jnp.clip(base // GROUP + group, 0, ids_ref.shape[0] - 1), 1), :]
        line = jnp.where(real, line, NO_LABEL)
        ids = jnp.transpose(jnp.broadcast_to(line, (GROUP, LANES)))
        used, bits = features(ids, lane, HD)
        x = xs[pl.ds(at, GROUP), :].astype(F32)
        y = ys[pl.ds(at, GROUP), :].astype(F32)
        q_side = jnp.where(used, -FAR * bits, 0.0)
        k_side = jnp.where(used, 1.0 - bits, 0.0)
        qa[pl.ds(at, GROUP), :] = jnp.where(low, x * (1.0 / math.sqrt(HD)), q_side).astype(BF16)
        ka[pl.ds(at, GROUP), :] = jnp.where(low, y, k_side).astype(BF16)
        xv[pl.ds(at, GROUP), :] = jnp.where(low, 0.0, x).astype(BF16)
        return carry

    lax.fori_loop(0, GROUPS, prepare, 0)
    _, bits = features(jnp.full((PAD, LANES), NO_LABEL, jnp.int32),
                       lax.broadcasted_iota(jnp.int32, (PAD, LANES), 1), HD)
    pad_lane = lax.broadcasted_iota(jnp.int32, (PAD, LANES), 1)
    pad_used = jnp.logical_and(pad_lane >= HD, pad_lane < HD + 2 * BITS)
    zero = jnp.zeros((PAD, LANES), BF16)
    qa[WINDOW:, :] = jnp.where(pad_used, -FAR * bits, 0.0).astype(BF16)
    ka[WINDOW:, :] = jnp.where(pad_used, 1.0 - bits, 0.0).astype(BF16)
    xv[WINDOW:, :] = zero
    xs[WINDOW:, :] = zero
    ys[WINDOW:, :] = zero
    lse[...] = jnp.zeros_like(lse)
    delta[pl.ds(GROUPS, delta.shape[0] - GROUPS), :] = jnp.zeros(
        (delta.shape[0] - GROUPS, LANES), F32
    )

    for block in range(BLOCKS):
        at = pl.multiple_of(BOARD + block * GROUP + parity * ROWS, ROWS)
        to = pl.ds(block * ROWS, ROWS)
        own_qa[to, :] = qa[pl.ds(at, ROWS), :]
        own_ka[to, :] = ka[pl.ds(at, ROWS), :]
        own_xv[to, :] = xv[pl.ds(at, ROWS), :]
        own_y[to, :] = ys[pl.ds(at, ROWS), :]

    first = starts[outer * BOARD_GROUPS] - base
    last = ends[outer * BOARD_GROUPS + BOARD_GROUPS - 1] - base
    tile_groups = QT // GROUP

    def chunks(lo, hi, size):
        begin = lo // GROUP * GROUP
        return begin, (hi - begin + size - 1) // size

    def totals(tile, carry):
        at = pl.multiple_of(tile * QT, QT)
        group = outer * BOARD_GROUPS - BOARD_GROUPS + tile * tile_groups
        group_top = starts.shape[0] - 1
        lo = jnp.maximum(starts[jnp.clip(group, 0, group_top)] - base, first)
        hi = jnp.minimum(ends[jnp.clip(group + tile_groups - 1, 0, group_top)] - base, last)
        begin, count = chunks(lo, hi, KT)
        queries = qa[pl.ds(at, QT), :]

        def step(num, state):
            top, total = state
            here = pl.multiple_of(begin + num * KT, GROUP)
            scores = rows_by_rows(ka[pl.ds(here, KT), :], queries).reshape(KT // 8, 8, QT)
            new_top = jnp.maximum(top, jnp.max(scores, axis=0))
            terms = jnp.sum(jnp.exp(scores - new_top[None]), axis=0)
            return new_top, total * jnp.exp(top - new_top) + terms

        top, total = lax.fori_loop(
            0, count, step, (jnp.full((8, QT), LOWEST, F32), jnp.zeros((8, QT), F32))
        )
        highest = jnp.max(top, axis=0, keepdims=True)
        line = highest + jnp.log(jnp.sum(total * jnp.exp(top - highest), axis=0, keepdims=True))
        line = jnp.where(highest < -0.5 * FAR, 0.0, line)
        for part in range(tile_groups):
            lse[pl.ds(tile * tile_groups + part, 1), :] = line[:, part * LANES : (part + 1) * LANES]
        return carry

    lax.fori_loop(first // QT, (last + QT - 1) // QT, totals, 0)

    tile_blocks = TILE // ROWS

    def own_columns(source, tile):
        columns = []
        for pair in range(tile_blocks // 2):
            group = BOARD_GROUPS + tile * tile_blocks + 2 * pair
            a, b = source[pl.ds(group, 1), :], source[pl.ds(group + 1, 1), :]
            line = jnp.where(
                low_row, jnp.where(swap, half_turn(a), a), jnp.where(swap, b, half_turn(b))
            )
            columns.append(jnp.transpose(jnp.broadcast_to(line, (GROUP, LANES))))
        return jnp.concatenate(columns, axis=0)

    def own_range(tile):
        group = outer * BOARD_GROUPS + tile * tile_blocks
        return chunks(starts[group] - base, ends[group + tile_blocks - 1] - base, KC)

    for tile in range(OWN // TILE):
        rows = slice(tile * TILE, (tile + 1) * TILE)
        begin, count = own_range(tile)
        logs = jnp.concatenate([own_columns(lse, tile)] * (KC // LANES), axis=1)
        drops = jnp.concatenate([own_columns(delta, tile)] * (KC // LANES), axis=1)
        acc[...] = jnp.zeros_like(acc)

        def step(num, carry):
            at = pl.multiple_of(begin + num * KC, GROUP)
            here = pl.ds(at, KC)
            weights = jnp.exp(rows_by_rows(own_qa[rows, :], ka[here, :]) - logs)
            grads = weights * (rows_by_rows(own_y[rows, :], xv[here, :]) - drops)
            acc[0] += rows_by_cols(grads.astype(BF16), ys[here, :])
            lines = [(begin + num * KC) // GROUP + part for part in range(KC // LANES)]
            logs_row = jnp.concatenate([lse[pl.ds(n, 1), :] for n in lines], axis=1)
            drops_row = jnp.concatenate([delta[pl.ds(n, 1), :] for n in lines], axis=1)
            weights = jnp.exp(rows_by_rows(own_ka[rows, :], qa[here, :]) - logs_row)
            grads = weights * (rows_by_rows(own_xv[rows, :], ys[here, :]) - drops_row)
            acc[1] += rows_by_cols(grads.astype(BF16), xs[here, :])
            acc[2] += rows_by_cols(weights.astype(BF16), ys[here, :])
            return carry

        lax.fori_loop(0, count, step, 0)
        dq = acc[0] * (1.0 / math.sqrt(HD))
        both = jnp.where(low_lanes(TILE), acc[1] * (1.0 / math.sqrt(HD)), acc[2]).astype(BF16)
        low_half = low_lanes(ROWS // 2)
        for block in range(tile_blocks):
            upper = dq[block * ROWS : block * ROWS + ROWS // 2]
            lower = dq[block * ROWS + ROWS // 2 : (block + 1) * ROWS]
            out_ref[tile * tile_blocks + block, ROWS:] = jnp.where(
                low_half, upper, half_turn(lower)
            ).astype(BF16)
            out_ref[tile * tile_blocks + block, :ROWS] = both[block * ROWS : (block + 1) * ROWS]


def main(meta, starts, ends, ids, pieces):
    smem = pl.BlockSpec(memory_space=pltpu.SMEM)
    vmem = pl.BlockSpec(memory_space=pltpu.VMEM)
    window = pltpu.VMEM((WINDOW + PAD, LANES), BF16)
    own = pltpu.VMEM((OWN, LANES), BF16)
    lines = pltpu.VMEM((GROUPS + 8 * (PAD // GROUP // 8 + 1), LANES), F32)
    return pl.pallas_call(
        main_kernel,
        out_shape=jax.ShapeDtypeStruct((BLOCKS, OUT_ROWS, LANES), BF16),
        in_specs=[smem, smem, smem, vmem] + [vmem] * 6,
        out_specs=vmem,
        scratch_shapes=[window] * 5 + [own] * 4 + [lines] * 2
        + [pltpu.VMEM((3, TILE, LANES), F32)],
        compiler_params=pltpu.CompilerParams(vmem_limit_bytes=32 * 1024 * 1024),
    )(meta, starts, ends, ids, *pieces)


def moved(x, boards, flip):
    heads, outers = lax.axis_size("head"), lax.axis_size("outer")
    pairs = [
        (h * outers + i, (h ^ flip) * outers + i + boards)
        for h in range(heads)
        for i in range(outers)
        if 0 <= i + boards < outers
    ]
    return lax.ppermute(x, ("head", "outer"), pairs)


def local(queries, keys, values, grad_out, saved_out, segment_ids):
    ids = segment_ids.reshape(-1, GROUP)
    starts = jnp.sum(segment_ids[None, :] < ids[:, :1], axis=1, dtype=jnp.int32)
    ends = jnp.sum(segment_ids[None, :] <= ids[:, -1:], axis=1, dtype=jnp.int32)
    meta = jnp.stack([lax.axis_index("outer"), lax.axis_index("inner"), lax.axis_index("head")])
    message = pack(queries, keys, values, grad_out, saved_out)
    mine = lax.all_to_all(message, "inner", split_axis=0, concat_axis=0, tiled=True)
    pieces = (
        mine,
        moved(mine, 0, 1),
        moved(mine, 1, 0),
        moved(mine, 1, 1),
        moved(mine, -1, 0),
        moved(mine, -1, 1),
    )
    results = main(meta, starts, ends, ids, pieces)
    gathered = lax.all_to_all(results, "inner", split_axis=0, concat_axis=0, tiled=True)
    return unpack(gathered)


def solution(mesh):
    rows = P(("outer", "inner", "head"), None)
    return jax.shard_map(
        local,
        mesh=mesh,
        in_specs=(rows, rows, rows, rows, rows, P()),
        out_specs=(rows, rows, rows),
        check_vma=False,
    )
```

```python
import math

import jax
import jax.numpy as jnp
from jax import lax
from jax.experimental import pallas as pl
from jax.experimental.pallas import tpu as pltpu
from jax.sharding import PartitionSpec as P

HD = 64
ROWS = 64
LANES = 128
BLOCKS = 8
MSG = 2 * ROWS + 16
OUT_ROWS = ROWS + ROWS // 2
BOARD = 1024
GROUP = 128
BOARD_GROUPS = BOARD // GROUP
WINDOW = 3 * BOARD
GROUPS = WINDOW // GROUP
OWN = BLOCKS * ROWS
QT = 512
KT = 512
KC = 768
TILE = 256
PAD = max(KC, KT)
FAR = 2.0**100
NO_LABEL = 63
BITS = 6
LOWEST = -3e38
F32 = jnp.float32
BF16 = jnp.bfloat16


def rows_by_rows(left, right):
    return lax.dot_general(left, right, (((1,), (1,)), ((), ())), preferred_element_type=F32)


def rows_by_cols(left, right):
    return lax.dot_general(left, right, (((1,), (0,)), ((), ())), preferred_element_type=F32)


def half_turn(x):
    return pltpu.roll(x, HD, axis=1)


def low_lanes(rows):
    return lax.broadcasted_iota(jnp.int32, (rows, LANES), 1) < HD


def pack_kernel(q_ref, k_ref, v_ref, g_ref, s_ref, out_ref):
    low = low_lanes(ROWS)
    for pair in range(4):
        cols = slice(pair * LANES, (pair + 1) * LANES)
        q, k, v, g = (r[:, cols].astype(F32) for r in (q_ref, k_ref, v_ref, g_ref))
        out_ref[2 * pair, :ROWS] = jnp.where(low, q, half_turn(v)).astype(BF16)
        out_ref[2 * pair + 1, :ROWS] = jnp.where(low, half_turn(q), v).astype(BF16)
        out_ref[2 * pair, ROWS : 2 * ROWS] = jnp.where(low, k, half_turn(g)).astype(BF16)
        out_ref[2 * pair + 1, ROWS : 2 * ROWS] = jnp.where(low, half_turn(k), g).astype(BF16)
    cols = 8 * HD
    products = g_ref[...].astype(F32) * s_ref[...].astype(F32)
    high = products.astype(BF16)
    rest = (products - high.astype(F32)).astype(BF16)
    head_of = lax.broadcasted_iota(jnp.int32, (16, cols), 1) // HD
    wanted = lax.broadcasted_iota(jnp.int32, (16, cols), 0) % 8
    pick = jnp.where(head_of == wanted, 1.0, 0.0).astype(BF16)
    twice = lambda x: jnp.concatenate([x, x], axis=0)
    deltas = rows_by_rows(pick, twice(high)) + rows_by_rows(pick, twice(rest))
    first = deltas.astype(BF16).astype(F32)
    second = (deltas - first).astype(BF16).astype(F32)
    third = deltas - first - second
    row = lax.broadcasted_iota(jnp.int32, (16, LANES), 0)
    lowest = low_lanes(16)
    table = jnp.where(
        row < 8, jnp.where(lowest, first, second), jnp.where(lowest, third, 0.0)
    ).astype(BF16)
    for head in range(8):
        out_ref[head, 2 * ROWS :] = table


def pack(queries, keys, values, grad_out, saved_out):
    return pl.pallas_call(
        pack_kernel,
        out_shape=jax.ShapeDtypeStruct((8, MSG, LANES), BF16),
    )(queries, keys, values, grad_out, saved_out)


def unpack_kernel(in_ref, dq_ref, dk_ref, dv_ref):
    low = low_lanes(ROWS)
    low_half = low_lanes(ROWS // 2)
    for pair in range(4):
        cols = slice(pair * LANES, (pair + 1) * LANES)
        a = in_ref[2 * pair, :ROWS].astype(F32)
        b = in_ref[2 * pair + 1, :ROWS].astype(F32)
        dk_ref[:, cols] = jnp.where(low, a, half_turn(b)).astype(BF16)
        dv_ref[:, cols] = jnp.where(low, half_turn(a), b).astype(BF16)
        c = in_ref[2 * pair, ROWS:].astype(F32)
        d = in_ref[2 * pair + 1, ROWS:].astype(F32)
        dq_ref[: ROWS // 2, cols] = jnp.where(low_half, c, half_turn(d)).astype(BF16)
        dq_ref[ROWS // 2 :, cols] = jnp.where(low_half, half_turn(c), d).astype(BF16)


def unpack(results):
    shape = jax.ShapeDtypeStruct((ROWS, 8 * HD), BF16)
    return pl.pallas_call(unpack_kernel, out_shape=(shape, shape, shape))(results)


def features(ids, lane, lead):
    at = lane - lead
    second = at >= BITS
    bit = lax.shift_right_logical(ids, jnp.where(second, at - BITS, at) & 31) & 1
    used = jnp.logical_and(at >= 0, at < 2 * BITS)
    return used, jnp.where(second, 1 - bit, bit).astype(F32)


def main_kernel(
    meta, starts, ends, ids_ref, p0, p1, p2, p3, p4, p5, out_ref,
    xs, ys, qa, ka, xv, own_qa, own_ka, own_xv, own_y, lse, delta, acc,
):
    outer, head, parity = meta[0], meta[1], meta[2]
    base = (outer - 1) * BOARD
    lane = lax.broadcasted_iota(jnp.int32, (GROUP, LANES), 1)
    low = lane < HD
    low_row = low_lanes(1)
    sub16 = lax.broadcasted_iota(jnp.int32, (16, LANES), 0)
    delta_rows = jnp.logical_or(sub16 == head, sub16 == head + 8)

    pieces = ((p2, p3), (p0, p1), (p4, p5))
    swap = parity == 1
    odd = outer % 2
    sides = ((parity + 1 + odd) % 2, parity, (parity + odd) % 2)
    for board in range(3):
        mine, other = pieces[board]
        mine_side = sides[board]
        for block in range(BLOCKS):
            group = board * BLOCKS + block
            for piece, side in ((mine, mine_side), (other, 1 - mine_side)):
                at = pl.multiple_of(group * GROUP + side * ROWS, ROWS)
                xs[pl.ds(at, ROWS), :] = piece[block, :ROWS]
                ys[pl.ds(at, ROWS), :] = piece[block, ROWS : 2 * ROWS]
            parts = []
            for piece in (mine, other):
                table = jnp.where(delta_rows, piece[block, 2 * ROWS :].astype(F32), 0.0)
                line = jnp.sum(table, axis=0, keepdims=True)
                parts.append(line + half_turn(line))
            delta[pl.ds(group, 1), :] = jnp.where(
                jnp.logical_xor(low_row, mine_side == 1), parts[0], parts[1]
            )

    def prepare(group, carry):
        at = pl.multiple_of(group * GROUP, GROUP)
        board = outer - 1 + group // BOARD_GROUPS
        real = jnp.logical_and(board >= 0, board < ids_ref.shape[0] // BOARD_GROUPS)
        line = ids_ref[pl.ds(jnp.clip(base // GROUP + group, 0, ids_ref.shape[0] - 1), 1), :]
        line = jnp.where(real, line, NO_LABEL)
        ids = jnp.transpose(jnp.broadcast_to(line, (GROUP, LANES)))
        used, bits = features(ids, lane, HD)
        x = xs[pl.ds(at, GROUP), :].astype(F32)
        y = ys[pl.ds(at, GROUP), :].astype(F32)
        q_side = jnp.where(used, -FAR * bits, 0.0)
        k_side = jnp.where(used, 1.0 - bits, 0.0)
        qa[pl.ds(at, GROUP), :] = jnp.where(low, x * (1.0 / math.sqrt(HD)), q_side).astype(BF16)
        ka[pl.ds(at, GROUP), :] = jnp.where(low, y, k_side).astype(BF16)
        xv[pl.ds(at, GROUP), :] = jnp.where(low, 0.0, x).astype(BF16)
        return carry

    lax.fori_loop(0, GROUPS, prepare, 0)
    _, bits = features(jnp.full((PAD, LANES), NO_LABEL, jnp.int32),
                       lax.broadcasted_iota(jnp.int32, (PAD, LANES), 1), HD)
    pad_lane = lax.broadcasted_iota(jnp.int32, (PAD, LANES), 1)
    pad_used = jnp.logical_and(pad_lane >= HD, pad_lane < HD + 2 * BITS)
    zero = jnp.zeros((PAD, LANES), BF16)
    qa[WINDOW:, :] = jnp.where(pad_used, -FAR * bits, 0.0).astype(BF16)
    ka[WINDOW:, :] = jnp.where(pad_used, 1.0 - bits, 0.0).astype(BF16)
    xv[WINDOW:, :] = zero
    xs[WINDOW:, :] = zero
    ys[WINDOW:, :] = zero
    lse[...] = jnp.zeros_like(lse)
    delta[pl.ds(GROUPS, delta.shape[0] - GROUPS), :] = jnp.zeros(
        (delta.shape[0] - GROUPS, LANES), F32
    )

    for block in range(BLOCKS):
        at = pl.multiple_of(BOARD + block * GROUP + parity * ROWS, ROWS)
        to = pl.ds(block * ROWS, ROWS)
        own_qa[to, :] = qa[pl.ds(at, ROWS), :]
        own_ka[to, :] = ka[pl.ds(at, ROWS), :]
        own_xv[to, :] = xv[pl.ds(at, ROWS), :]
        own_y[to, :] = ys[pl.ds(at, ROWS), :]

    first = starts[outer * BOARD_GROUPS] - base
    last = ends[outer * BOARD_GROUPS + BOARD_GROUPS - 1] - base
    tile_groups = QT // GROUP

    def chunks(lo, hi, size):
        begin = lo // GROUP * GROUP
        return begin, (hi - begin + size - 1) // size

    def totals(tile, carry):
        at = pl.multiple_of(tile * QT, QT)
        group = outer * BOARD_GROUPS - BOARD_GROUPS + tile * tile_groups
        group_top = starts.shape[0] - 1
        lo = jnp.maximum(starts[jnp.clip(group, 0, group_top)] - base, first)
        hi = jnp.minimum(ends[jnp.clip(group + tile_groups - 1, 0, group_top)] - base, last)
        begin, count = chunks(lo, hi, KT)
        queries = qa[pl.ds(at, QT), :]

        def step(num, state):
            top, total = state
            here = pl.multiple_of(begin + num * KT, GROUP)
            scores = rows_by_rows(ka[pl.ds(here, KT), :], queries).reshape(KT // 8, 8, QT)
            new_top = jnp.maximum(top, jnp.max(scores, axis=0))
            terms = jnp.sum(jnp.exp(scores - new_top[None]), axis=0)
            return new_top, total * jnp.exp(top - new_top) + terms

        top, total = lax.fori_loop(
            0, count, step, (jnp.full((8, QT), LOWEST, F32), jnp.zeros((8, QT), F32))
        )
        highest = jnp.max(top, axis=0, keepdims=True)
        line = highest + jnp.log(jnp.sum(total * jnp.exp(top - highest), axis=0, keepdims=True))
        line = jnp.where(highest < -0.5 * FAR, 0.0, line)
        for part in range(tile_groups):
            lse[pl.ds(tile * tile_groups + part, 1), :] = line[:, part * LANES : (part + 1) * LANES]
        return carry

    lax.fori_loop(first // QT, (last + QT - 1) // QT, totals, 0)

    tile_blocks = TILE // ROWS

    def own_columns(source, tile):
        columns = []
        for pair in range(tile_blocks // 2):
            group = BOARD_GROUPS + tile * tile_blocks + 2 * pair
            a, b = source[pl.ds(group, 1), :], source[pl.ds(group + 1, 1), :]
            line = jnp.where(
                low_row, jnp.where(swap, half_turn(a), a), jnp.where(swap, b, half_turn(b))
            )
            columns.append(jnp.transpose(jnp.broadcast_to(line, (GROUP, LANES))))
        return jnp.concatenate(columns, axis=0)

    def own_range(tile):
        group = outer * BOARD_GROUPS + tile * tile_blocks
        return chunks(starts[group] - base, ends[group + tile_blocks - 1] - base, KC)

    for tile in range(OWN // TILE):
        rows = slice(tile * TILE, (tile + 1) * TILE)
        begin, count = own_range(tile)
        logs = jnp.concatenate([own_columns(lse, tile)] * (KC // LANES), axis=1)
        drops = jnp.concatenate([own_columns(delta, tile)] * (KC // LANES), axis=1)
        acc[...] = jnp.zeros_like(acc)

        def step(num, carry):
            at = pl.multiple_of(begin + num * KC, GROUP)
            here = pl.ds(at, KC)
            weights = jnp.exp(rows_by_rows(own_qa[rows, :], ka[here, :]) - logs)
            grads = weights * (rows_by_rows(own_y[rows, :], xv[here, :]) - drops)
            acc[0] += rows_by_cols(grads.astype(BF16), ys[here, :])
            lines = [(begin + num * KC) // GROUP + part for part in range(KC // LANES)]
            logs_row = jnp.concatenate([lse[pl.ds(n, 1), :] for n in lines], axis=1)
            drops_row = jnp.concatenate([delta[pl.ds(n, 1), :] for n in lines], axis=1)
            weights = jnp.exp(rows_by_rows(own_ka[rows, :], qa[here, :]) - logs_row)
            grads = weights * (rows_by_rows(own_xv[rows, :], ys[here, :]) - drops_row)
            acc[1] += rows_by_cols(grads.astype(BF16), xs[here, :])
            acc[2] += rows_by_cols(weights.astype(BF16), ys[here, :])
            return carry

        lax.fori_loop(0, count, step, 0)
        dq = acc[0] * (1.0 / math.sqrt(HD))
        both = jnp.where(low_lanes(TILE), acc[1] * (1.0 / math.sqrt(HD)), acc[2]).astype(BF16)
        low_half = low_lanes(ROWS // 2)
        for block in range(tile_blocks):
            upper = dq[block * ROWS : block * ROWS + ROWS // 2]
            lower = dq[block * ROWS + ROWS // 2 : (block + 1) * ROWS]
            out_ref[tile * tile_blocks + block, ROWS:] = jnp.where(
                low_half, upper, half_turn(lower)
            ).astype(BF16)
            out_ref[tile * tile_blocks + block, :ROWS] = both[block * ROWS : (block + 1) * ROWS]


def main(meta, starts, ends, ids, pieces):
    smem = pl.BlockSpec(memory_space=pltpu.SMEM)
    vmem = pl.BlockSpec(memory_space=pltpu.VMEM)
    window = pltpu.VMEM((WINDOW + PAD, LANES), BF16)
    own = pltpu.VMEM((OWN, LANES), BF16)
    lines = pltpu.VMEM((GROUPS + 8 * (PAD // GROUP // 8 + 1), LANES), F32)
    return pl.pallas_call(
        main_kernel,
        out_shape=jax.ShapeDtypeStruct((BLOCKS, OUT_ROWS, LANES), BF16),
        in_specs=[smem, smem, smem, vmem] + [vmem] * 6,
        out_specs=vmem,
        scratch_shapes=[window] * 5 + [own] * 4 + [lines] * 2
        + [pltpu.VMEM((3, TILE, LANES), F32)],
        compiler_params=pltpu.CompilerParams(vmem_limit_bytes=32 * 1024 * 1024),
    )(meta, starts, ends, ids, *pieces)


def from_partner(x):
    return lax.ppermute(x, "head", [(h, 1 - h) for h in range(lax.axis_size("head"))])


def from_board(x, boards):
    heads, outers = lax.axis_size("head"), lax.axis_size("outer")
    pairs = []
    for h in range(heads):
        for i in range(outers):
            if 0 <= i + boards < outers:
                to_head = h if i // 2 == (i + boards) // 2 else 1 - h
                pairs.append((h * outers + i, to_head * outers + i + boards))
    return lax.ppermute(x, ("head", "outer"), pairs)


def local(queries, keys, values, grad_out, saved_out, segment_ids):
    ids = segment_ids.reshape(-1, GROUP)
    starts = jnp.sum(segment_ids[None, :] < ids[:, :1], axis=1, dtype=jnp.int32)
    ends = jnp.sum(segment_ids[None, :] <= ids[:, -1:], axis=1, dtype=jnp.int32)
    meta = jnp.stack([lax.axis_index("outer"), lax.axis_index("inner"), lax.axis_index("head")])
    message = pack(queries, keys, values, grad_out, saved_out)
    mine = lax.all_to_all(message, "inner", split_axis=0, concat_axis=0, tiled=True)
    theirs = from_partner(mine)
    pieces = (
        mine,
        theirs,
        from_board(mine, 1),
        from_board(theirs, 1),
        from_board(mine, -1),
        from_board(theirs, -1),
    )
    results = main(meta, starts, ends, ids, pieces)
    gathered = lax.all_to_all(results, "inner", split_axis=0, concat_axis=0, tiled=True)
    return unpack(gathered)


def solution(mesh):
    rows = P(("outer", "inner", "head"), None)
    return jax.shard_map(
        local,
        mesh=mesh,
        in_specs=(rows, rows, rows, rows, rows, P()),
        out_specs=(rows, rows, rows),
        check_vma=False,
    )
```

```python
import math

import jax
import jax.numpy as jnp
from jax import lax
from jax.experimental import pallas as pl
from jax.experimental.pallas import tpu as pltpu
from jax.sharding import PartitionSpec as P

HD = 64
ROWS = 64
LANES = 128
BLOCKS = 8
MSG = 2 * ROWS + 16
OUT_ROWS = ROWS + ROWS // 2
BOARD = 1024
GROUP = 128
BOARD_GROUPS = BOARD // GROUP
WINDOW = 3 * BOARD
GROUPS = WINDOW // GROUP
OWN = BLOCKS * ROWS
QT = 512
KT = 640
SUB = 128
KC = 768
TILE = 256
PAD = max(KC, KT)
FAR = 2.0**100
NO_LABEL = 63
BITS = 6
LOWEST = -3e38
F32 = jnp.float32
BF16 = jnp.bfloat16


def rows_by_rows(left, right):
    return lax.dot_general(left, right, (((1,), (1,)), ((), ())), preferred_element_type=F32)


def rows_by_cols(left, right):
    return lax.dot_general(left, right, (((1,), (0,)), ((), ())), preferred_element_type=F32)


def half_turn(x):
    return pltpu.roll(x, HD, axis=1)


def low_lanes(rows):
    return lax.broadcasted_iota(jnp.int32, (rows, LANES), 1) < HD


def pack_kernel(q_ref, k_ref, v_ref, g_ref, s_ref, out_ref):
    low = low_lanes(ROWS)
    for pair in range(4):
        cols = slice(pair * LANES, (pair + 1) * LANES)
        q, k, v, g = (r[:, cols].astype(F32) for r in (q_ref, k_ref, v_ref, g_ref))
        out_ref[2 * pair, :ROWS] = jnp.where(low, q, half_turn(v)).astype(BF16)
        out_ref[2 * pair + 1, :ROWS] = jnp.where(low, half_turn(q), v).astype(BF16)
        out_ref[2 * pair, ROWS : 2 * ROWS] = jnp.where(low, k, half_turn(g)).astype(BF16)
        out_ref[2 * pair + 1, ROWS : 2 * ROWS] = jnp.where(low, half_turn(k), g).astype(BF16)
    cols = 8 * HD
    products = g_ref[...].astype(F32) * s_ref[...].astype(F32)
    high = products.astype(BF16)
    rest = (products - high.astype(F32)).astype(BF16)
    head_of = lax.broadcasted_iota(jnp.int32, (16, cols), 1) // HD
    wanted = lax.broadcasted_iota(jnp.int32, (16, cols), 0) % 8
    pick = jnp.where(head_of == wanted, 1.0, 0.0).astype(BF16)
    twice = lambda x: jnp.concatenate([x, x], axis=0)
    deltas = rows_by_rows(pick, twice(high)) + rows_by_rows(pick, twice(rest))
    first = deltas.astype(BF16).astype(F32)
    second = (deltas - first).astype(BF16).astype(F32)
    third = deltas - first - second
    row = lax.broadcasted_iota(jnp.int32, (16, LANES), 0)
    lowest = low_lanes(16)
    table = jnp.where(
        row < 8, jnp.where(lowest, first, second), jnp.where(lowest, third, 0.0)
    ).astype(BF16)
    for head in range(8):
        out_ref[head, 2 * ROWS :] = table


def pack(queries, keys, values, grad_out, saved_out):
    return pl.pallas_call(
        pack_kernel,
        out_shape=jax.ShapeDtypeStruct((8, MSG, LANES), BF16),
    )(queries, keys, values, grad_out, saved_out)


def unpack_kernel(in_ref, dq_ref, dk_ref, dv_ref):
    low = low_lanes(ROWS)
    low_half = low_lanes(ROWS // 2)
    for pair in range(4):
        cols = slice(pair * LANES, (pair + 1) * LANES)
        a = in_ref[2 * pair, :ROWS].astype(F32)
        b = in_ref[2 * pair + 1, :ROWS].astype(F32)
        dk_ref[:, cols] = jnp.where(low, a, half_turn(b)).astype(BF16)
        dv_ref[:, cols] = jnp.where(low, half_turn(a), b).astype(BF16)
        c = in_ref[2 * pair, ROWS:].astype(F32)
        d = in_ref[2 * pair + 1, ROWS:].astype(F32)
        dq_ref[: ROWS // 2, cols] = jnp.where(low_half, c, half_turn(d)).astype(BF16)
        dq_ref[ROWS // 2 :, cols] = jnp.where(low_half, half_turn(c), d).astype(BF16)


def unpack(results):
    shape = jax.ShapeDtypeStruct((ROWS, 8 * HD), BF16)
    return pl.pallas_call(unpack_kernel, out_shape=(shape, shape, shape))(results)


def features(ids, lane, lead):
    at = lane - lead
    second = at >= BITS
    bit = lax.shift_right_logical(ids, jnp.where(second, at - BITS, at) & 31) & 1
    used = jnp.logical_and(at >= 0, at < 2 * BITS)
    return used, jnp.where(second, 1 - bit, bit).astype(F32)


def main_kernel(
    meta, starts, ends, ids_ref, p0, p1, p2, p3, p4, p5, out_ref,
    xs, ys, qa, ka, xv, own_qa, own_ka, own_xv, own_y, lse, delta, acc,
):
    outer, head, parity = meta[0], meta[1], meta[2]
    base = (outer - 1) * BOARD
    lane = lax.broadcasted_iota(jnp.int32, (GROUP, LANES), 1)
    low = lane < HD
    low_row = low_lanes(1)
    sub16 = lax.broadcasted_iota(jnp.int32, (16, LANES), 0)
    delta_rows = jnp.logical_or(sub16 == head, sub16 == head + 8)

    pieces = ((p2, p3), (p0, p1), (p4, p5))
    swap = parity == 1
    odd = outer % 2
    sides = ((parity + 1 + odd) % 2, parity, (parity + odd) % 2)
    for board in range(3):
        mine, other = pieces[board]
        mine_side = sides[board]
        for block in range(BLOCKS):
            group = board * BLOCKS + block
            for piece, side in ((mine, mine_side), (other, 1 - mine_side)):
                at = pl.multiple_of(group * GROUP + side * ROWS, ROWS)
                xs[pl.ds(at, ROWS), :] = piece[block, :ROWS]
                ys[pl.ds(at, ROWS), :] = piece[block, ROWS : 2 * ROWS]
            parts = []
            for piece in (mine, other):
                table = jnp.where(delta_rows, piece[block, 2 * ROWS :].astype(F32), 0.0)
                line = jnp.sum(table, axis=0, keepdims=True)
                parts.append(line + half_turn(line))
            delta[pl.ds(group, 1), :] = jnp.where(
                jnp.logical_xor(low_row, mine_side == 1), parts[0], parts[1]
            )

    def prepare(group, carry):
        at = pl.multiple_of(group * GROUP, GROUP)
        board = outer - 1 + group // BOARD_GROUPS
        real = jnp.logical_and(board >= 0, board < ids_ref.shape[0] // BOARD_GROUPS)
        line = ids_ref[pl.ds(jnp.clip(base // GROUP + group, 0, ids_ref.shape[0] - 1), 1), :]
        line = jnp.where(real, line, NO_LABEL)
        ids = jnp.transpose(jnp.broadcast_to(line, (GROUP, LANES)))
        used, bits = features(ids, lane, HD)
        x = xs[pl.ds(at, GROUP), :].astype(F32)
        y = ys[pl.ds(at, GROUP), :].astype(F32)
        q_side = jnp.where(used, -FAR * bits, 0.0)
        k_side = jnp.where(used, 1.0 - bits, 0.0)
        qa[pl.ds(at, GROUP), :] = jnp.where(low, x * (1.0 / math.sqrt(HD)), q_side).astype(BF16)
        ka[pl.ds(at, GROUP), :] = jnp.where(low, y, k_side).astype(BF16)
        xv[pl.ds(at, GROUP), :] = jnp.where(low, 0.0, x).astype(BF16)
        return carry

    lax.fori_loop(0, GROUPS, prepare, 0, unroll=12)
    _, bits = features(jnp.full((PAD, LANES), NO_LABEL, jnp.int32),
                       lax.broadcasted_iota(jnp.int32, (PAD, LANES), 1), HD)
    pad_lane = lax.broadcasted_iota(jnp.int32, (PAD, LANES), 1)
    pad_used = jnp.logical_and(pad_lane >= HD, pad_lane < HD + 2 * BITS)
    zero = jnp.zeros((PAD, LANES), BF16)
    qa[WINDOW:, :] = jnp.where(pad_used, -FAR * bits, 0.0).astype(BF16)
    ka[WINDOW:, :] = jnp.where(pad_used, 1.0 - bits, 0.0).astype(BF16)
    xv[WINDOW:, :] = zero
    xs[WINDOW:, :] = zero
    ys[WINDOW:, :] = zero
    lse[...] = jnp.zeros_like(lse)
    delta[pl.ds(GROUPS, delta.shape[0] - GROUPS), :] = jnp.zeros(
        (delta.shape[0] - GROUPS, LANES), F32
    )

    for block in range(BLOCKS):
        at = pl.multiple_of(BOARD + block * GROUP + parity * ROWS, ROWS)
        to = pl.ds(block * ROWS, ROWS)
        own_qa[to, :] = qa[pl.ds(at, ROWS), :]
        own_ka[to, :] = ka[pl.ds(at, ROWS), :]
        own_xv[to, :] = xv[pl.ds(at, ROWS), :]
        own_y[to, :] = ys[pl.ds(at, ROWS), :]

    first = starts[outer * BOARD_GROUPS] - base
    last = ends[outer * BOARD_GROUPS + BOARD_GROUPS - 1] - base
    tile_groups = QT // GROUP

    def chunks(lo, hi, size):
        begin = lo // GROUP * GROUP
        return begin, (hi - begin + size - 1) // size

    def totals(tile, carry):
        at = pl.multiple_of(tile * QT, QT)
        group = outer * BOARD_GROUPS - BOARD_GROUPS + tile * tile_groups
        group_top = starts.shape[0] - 1
        lo = jnp.maximum(starts[jnp.clip(group, 0, group_top)] - base, first)
        hi = jnp.minimum(ends[jnp.clip(group + tile_groups - 1, 0, group_top)] - base, last)
        begin, count = chunks(lo, hi, KT)
        queries = qa[pl.ds(at, QT), :]

        def step(num, state):
            top, total = state
            for part in range(KT // SUB):
                here = pl.multiple_of(begin + num * KT + part * SUB, GROUP)
                scores = rows_by_rows(ka[pl.ds(here, SUB), :], queries).reshape(SUB // 8, 8, QT)
                new_top = jnp.maximum(top, jnp.max(scores, axis=0))
                terms = jnp.sum(jnp.exp(scores - new_top[None]), axis=0)
                total = total * jnp.exp(top - new_top) + terms
                top = new_top
            return top, total

        top, total = lax.fori_loop(
            0, count, step, (jnp.full((8, QT), LOWEST, F32), jnp.zeros((8, QT), F32))
        )
        highest = jnp.max(top, axis=0, keepdims=True)
        line = highest + jnp.log(jnp.sum(total * jnp.exp(top - highest), axis=0, keepdims=True))
        line = jnp.where(highest < -0.5 * FAR, 0.0, line)
        for part in range(tile_groups):
            lse[pl.ds(tile * tile_groups + part, 1), :] = line[:, part * LANES : (part + 1) * LANES]
        return carry

    lax.fori_loop(first // QT, (last + QT - 1) // QT, totals, 0)

    tile_blocks = TILE // ROWS

    def own_columns(source, tile):
        columns = []
        for pair in range(tile_blocks // 2):
            group = BOARD_GROUPS + tile * tile_blocks + 2 * pair
            a, b = source[pl.ds(group, 1), :], source[pl.ds(group + 1, 1), :]
            line = jnp.where(
                low_row, jnp.where(swap, half_turn(a), a), jnp.where(swap, b, half_turn(b))
            )
            columns.append(jnp.transpose(jnp.broadcast_to(line, (GROUP, LANES))))
        return jnp.concatenate(columns, axis=0)

    def own_range(tile):
        group = outer * BOARD_GROUPS + tile * tile_blocks
        return chunks(starts[group] - base, ends[group + tile_blocks - 1] - base, KC)

    for tile in range(OWN // TILE):
        rows = slice(tile * TILE, (tile + 1) * TILE)
        begin, count = own_range(tile)
        logs = jnp.concatenate([own_columns(lse, tile)] * (KC // LANES), axis=1)
        drops = jnp.concatenate([own_columns(delta, tile)] * (KC // LANES), axis=1)
        acc[...] = jnp.zeros_like(acc)

        def step(num, carry):
            at = pl.multiple_of(begin + num * KC, GROUP)
            here = pl.ds(at, KC)
            weights = jnp.exp(rows_by_rows(own_qa[rows, :], ka[here, :]) - logs)
            grads = weights * (rows_by_rows(own_y[rows, :], xv[here, :]) - drops)
            acc[0] += rows_by_cols(grads.astype(BF16), ys[here, :])
            lines = [(begin + num * KC) // GROUP + part for part in range(KC // LANES)]
            logs_row = jnp.concatenate([lse[pl.ds(n, 1), :] for n in lines], axis=1)
            drops_row = jnp.concatenate([delta[pl.ds(n, 1), :] for n in lines], axis=1)
            weights = jnp.exp(rows_by_rows(own_ka[rows, :], qa[here, :]) - logs_row)
            grads = weights * (rows_by_rows(own_xv[rows, :], ys[here, :]) - drops_row)
            acc[1] += rows_by_cols(grads.astype(BF16), xs[here, :])
            acc[2] += rows_by_cols(weights.astype(BF16), ys[here, :])
            return carry

        lax.fori_loop(0, count, step, 0)
        dq = acc[0] * (1.0 / math.sqrt(HD))
        both = jnp.where(low_lanes(TILE), acc[1] * (1.0 / math.sqrt(HD)), acc[2]).astype(BF16)
        low_half = low_lanes(ROWS // 2)
        for block in range(tile_blocks):
            upper = dq[block * ROWS : block * ROWS + ROWS // 2]
            lower = dq[block * ROWS + ROWS // 2 : (block + 1) * ROWS]
            out_ref[tile * tile_blocks + block, ROWS:] = jnp.where(
                low_half, upper, half_turn(lower)
            ).astype(BF16)
            out_ref[tile * tile_blocks + block, :ROWS] = both[block * ROWS : (block + 1) * ROWS]


def main(meta, starts, ends, ids, pieces):
    smem = pl.BlockSpec(memory_space=pltpu.SMEM)
    vmem = pl.BlockSpec(memory_space=pltpu.VMEM)
    window = pltpu.VMEM((WINDOW + PAD, LANES), BF16)
    own = pltpu.VMEM((OWN, LANES), BF16)
    lines = pltpu.VMEM((GROUPS + 8 * (PAD // GROUP // 8 + 1), LANES), F32)
    return pl.pallas_call(
        main_kernel,
        out_shape=jax.ShapeDtypeStruct((BLOCKS, OUT_ROWS, LANES), BF16),
        in_specs=[smem, smem, smem, vmem] + [vmem] * 6,
        out_specs=vmem,
        scratch_shapes=[window] * 5 + [own] * 4 + [lines] * 2
        + [pltpu.VMEM((3, TILE, LANES), F32)],
        compiler_params=pltpu.CompilerParams(vmem_limit_bytes=32 * 1024 * 1024),
    )(meta, starts, ends, ids, *pieces)


def from_partner(x):
    return lax.ppermute(x, "head", [(h, 1 - h) for h in range(lax.axis_size("head"))])


def from_board(x, boards):
    heads, outers = lax.axis_size("head"), lax.axis_size("outer")
    pairs = []
    for h in range(heads):
        for i in range(outers):
            if 0 <= i + boards < outers:
                to_head = h if i // 2 == (i + boards) // 2 else 1 - h
                pairs.append((h * outers + i, to_head * outers + i + boards))
    return lax.ppermute(x, ("head", "outer"), pairs)


def local(queries, keys, values, grad_out, saved_out, segment_ids):
    ids = segment_ids.reshape(-1, GROUP)
    starts = jnp.sum(segment_ids[None, :] < ids[:, :1], axis=1, dtype=jnp.int32)
    ends = jnp.sum(segment_ids[None, :] <= ids[:, -1:], axis=1, dtype=jnp.int32)
    meta = jnp.stack([lax.axis_index("outer"), lax.axis_index("inner"), lax.axis_index("head")])
    message = pack(queries, keys, values, grad_out, saved_out)
    mine = lax.all_to_all(message, "inner", split_axis=0, concat_axis=0, tiled=True)
    theirs = from_partner(mine)
    pieces = (
        mine,
        theirs,
        from_board(mine, 1),
        from_board(theirs, 1),
        from_board(mine, -1),
        from_board(theirs, -1),
    )
    results = main(meta, starts, ends, ids, pieces)
    gathered = lax.all_to_all(results, "inner", split_axis=0, concat_axis=0, tiled=True)
    return unpack(gathered)


def solution(mesh):
    rows = P(("outer", "inner", "head"), None)
    return jax.shard_map(
        local,
        mesh=mesh,
        in_specs=(rows, rows, rows, rows, rows, P()),
        out_specs=(rows, rows, rows),
        check_vma=False,
    )
```

```python
import math

import jax
import jax.numpy as jnp
from jax import lax
from jax.experimental import pallas as pl
from jax.experimental.pallas import tpu as pltpu
from jax.sharding import PartitionSpec as P

HD = 64
ROWS = 64
LANES = 128
BLOCKS = 8
MSG = 2 * ROWS + 16
OUT_ROWS = ROWS + ROWS // 2
BOARD = 1024
GROUP = 128
BOARD_GROUPS = BOARD // GROUP
WINDOW = 3 * BOARD
GROUPS = WINDOW // GROUP
OWN = BLOCKS * ROWS
QT = 512
KT = 640
SUB = 128
KC = 768
TILE = 256
PAD = max(KC, KT)
FAR = 2.0**100
NO_LABEL = 63
BITS = 6
LOWEST = -3e38
F32 = jnp.float32
BF16 = jnp.bfloat16


def rows_by_rows(left, right):
    return lax.dot_general(left, right, (((1,), (1,)), ((), ())), preferred_element_type=F32)


def rows_by_cols(left, right):
    return lax.dot_general(left, right, (((1,), (0,)), ((), ())), preferred_element_type=F32)


def half_turn(x):
    return pltpu.roll(x, HD, axis=1)


def low_lanes(rows):
    return lax.broadcasted_iota(jnp.int32, (rows, LANES), 1) < HD


def pack_kernel(q_ref, k_ref, v_ref, g_ref, s_ref, out_ref):
    low = low_lanes(ROWS)
    for pair in range(4):
        cols = slice(pair * LANES, (pair + 1) * LANES)
        q, k, v, g = (r[:, cols].astype(F32) for r in (q_ref, k_ref, v_ref, g_ref))
        out_ref[2 * pair, :ROWS] = jnp.where(low, q, half_turn(v)).astype(BF16)
        out_ref[2 * pair + 1, :ROWS] = jnp.where(low, half_turn(q), v).astype(BF16)
        out_ref[2 * pair, ROWS : 2 * ROWS] = jnp.where(low, k, half_turn(g)).astype(BF16)
        out_ref[2 * pair + 1, ROWS : 2 * ROWS] = jnp.where(low, half_turn(k), g).astype(BF16)
    cols = 8 * HD
    products = g_ref[...].astype(F32) * s_ref[...].astype(F32)
    high = products.astype(BF16)
    rest = (products - high.astype(F32)).astype(BF16)
    head_of = lax.broadcasted_iota(jnp.int32, (16, cols), 1) // HD
    wanted = lax.broadcasted_iota(jnp.int32, (16, cols), 0) % 8
    pick = jnp.where(head_of == wanted, 1.0, 0.0).astype(BF16)
    twice = lambda x: jnp.concatenate([x, x], axis=0)
    deltas = rows_by_rows(pick, twice(high)) + rows_by_rows(pick, twice(rest))
    first = deltas.astype(BF16).astype(F32)
    second = (deltas - first).astype(BF16).astype(F32)
    third = deltas - first - second
    row = lax.broadcasted_iota(jnp.int32, (16, LANES), 0)
    lowest = low_lanes(16)
    table = jnp.where(
        row < 8, jnp.where(lowest, first, second), jnp.where(lowest, third, 0.0)
    ).astype(BF16)
    for head in range(8):
        out_ref[head, 2 * ROWS :] = table


def pack(queries, keys, values, grad_out, saved_out):
    return pl.pallas_call(
        pack_kernel,
        out_shape=jax.ShapeDtypeStruct((8, MSG, LANES), BF16),
    )(queries, keys, values, grad_out, saved_out)


def unpack_kernel(in_ref, dq_ref, dk_ref, dv_ref):
    low = low_lanes(ROWS)
    low_half = low_lanes(ROWS // 2)
    for pair in range(4):
        cols = slice(pair * LANES, (pair + 1) * LANES)
        a = in_ref[2 * pair, :ROWS].astype(F32)
        b = in_ref[2 * pair + 1, :ROWS].astype(F32)
        dk_ref[:, cols] = jnp.where(low, a, half_turn(b)).astype(BF16)
        dv_ref[:, cols] = jnp.where(low, half_turn(a), b).astype(BF16)
        c = in_ref[2 * pair, ROWS:].astype(F32)
        d = in_ref[2 * pair + 1, ROWS:].astype(F32)
        dq_ref[: ROWS // 2, cols] = jnp.where(low_half, c, half_turn(d)).astype(BF16)
        dq_ref[ROWS // 2 :, cols] = jnp.where(low_half, half_turn(c), d).astype(BF16)


def unpack(results):
    shape = jax.ShapeDtypeStruct((ROWS, 8 * HD), BF16)
    return pl.pallas_call(unpack_kernel, out_shape=(shape, shape, shape))(results)


def features(ids, lane, lead):
    at = lane - lead
    second = at >= BITS
    bit = lax.shift_right_logical(ids, jnp.where(second, at - BITS, at) & 31) & 1
    used = jnp.logical_and(at >= 0, at < 2 * BITS)
    return used, jnp.where(second, 1 - bit, bit).astype(F32)


def main_kernel(
    meta, starts, ends, ids_ref, p0, p1, p2, p3, p4, p5, out_ref,
    xs, ys, qa, ka, xv, own_qa, own_ka, own_xv, own_y, lse, delta, acc,
):
    outer, head, parity = meta[0], meta[1], meta[2]
    base = (outer - 1) * BOARD
    lane = lax.broadcasted_iota(jnp.int32, (GROUP, LANES), 1)
    low = lane < HD
    low_row = low_lanes(1)
    sub16 = lax.broadcasted_iota(jnp.int32, (16, LANES), 0)
    delta_rows = jnp.logical_or(sub16 == head, sub16 == head + 8)

    swap = parity == 1
    odd = outer % 2
    placed = (
        (1, p0, p1, parity),
        (2 - 2 * odd, p2, p3, parity),
        (2 * odd, p4, p5, 1 - parity),
    )
    for board, mine, other, mine_side in placed:
        for block in range(BLOCKS):
            group = board * BLOCKS + block
            for piece, side in ((mine, mine_side), (other, 1 - mine_side)):
                at = pl.multiple_of(group * GROUP + side * ROWS, ROWS)
                xs[pl.ds(at, ROWS), :] = piece[block, :ROWS]
                ys[pl.ds(at, ROWS), :] = piece[block, ROWS : 2 * ROWS]
            parts = []
            for piece in (mine, other):
                table = jnp.where(delta_rows, piece[block, 2 * ROWS :].astype(F32), 0.0)
                line = jnp.sum(table, axis=0, keepdims=True)
                parts.append(line + half_turn(line))
            delta[pl.ds(group, 1), :] = jnp.where(
                jnp.logical_xor(low_row, mine_side == 1), parts[0], parts[1]
            )

    def prepare(group, carry):
        at = pl.multiple_of(group * GROUP, GROUP)
        board = outer - 1 + group // BOARD_GROUPS
        real = jnp.logical_and(board >= 0, board < ids_ref.shape[0] // BOARD_GROUPS)
        line = ids_ref[pl.ds(jnp.clip(base // GROUP + group, 0, ids_ref.shape[0] - 1), 1), :]
        line = jnp.where(real, line, NO_LABEL)
        ids = jnp.transpose(jnp.broadcast_to(line, (GROUP, LANES)))
        used, bits = features(ids, lane, HD)
        x = xs[pl.ds(at, GROUP), :].astype(F32)
        y = ys[pl.ds(at, GROUP), :].astype(F32)
        q_side = jnp.where(used, -FAR * bits, 0.0)
        k_side = jnp.where(used, 1.0 - bits, 0.0)
        qa[pl.ds(at, GROUP), :] = jnp.where(low, x * (1.0 / math.sqrt(HD)), q_side).astype(BF16)
        ka[pl.ds(at, GROUP), :] = jnp.where(low, y, k_side).astype(BF16)
        xv[pl.ds(at, GROUP), :] = jnp.where(low, 0.0, x).astype(BF16)
        return carry

    lax.fori_loop(0, GROUPS, prepare, 0, unroll=12)
    _, bits = features(jnp.full((PAD, LANES), NO_LABEL, jnp.int32),
                       lax.broadcasted_iota(jnp.int32, (PAD, LANES), 1), HD)
    pad_lane = lax.broadcasted_iota(jnp.int32, (PAD, LANES), 1)
    pad_used = jnp.logical_and(pad_lane >= HD, pad_lane < HD + 2 * BITS)
    zero = jnp.zeros((PAD, LANES), BF16)
    qa[WINDOW:, :] = jnp.where(pad_used, -FAR * bits, 0.0).astype(BF16)
    ka[WINDOW:, :] = jnp.where(pad_used, 1.0 - bits, 0.0).astype(BF16)
    xv[WINDOW:, :] = zero
    xs[WINDOW:, :] = zero
    ys[WINDOW:, :] = zero
    lse[...] = jnp.zeros_like(lse)
    delta[pl.ds(GROUPS, delta.shape[0] - GROUPS), :] = jnp.zeros(
        (delta.shape[0] - GROUPS, LANES), F32
    )

    for block in range(BLOCKS):
        at = pl.multiple_of(BOARD + block * GROUP + parity * ROWS, ROWS)
        to = pl.ds(block * ROWS, ROWS)
        own_qa[to, :] = qa[pl.ds(at, ROWS), :]
        own_ka[to, :] = ka[pl.ds(at, ROWS), :]
        own_xv[to, :] = xv[pl.ds(at, ROWS), :]
        own_y[to, :] = ys[pl.ds(at, ROWS), :]

    first = starts[outer * BOARD_GROUPS] - base
    last = ends[outer * BOARD_GROUPS + BOARD_GROUPS - 1] - base
    tile_groups = QT // GROUP

    def chunks(lo, hi, size):
        begin = lo // GROUP * GROUP
        return begin, (hi - begin + size - 1) // size

    def totals(tile, carry):
        at = pl.multiple_of(tile * QT, QT)
        group = outer * BOARD_GROUPS - BOARD_GROUPS + tile * tile_groups
        group_top = starts.shape[0] - 1
        lo = jnp.maximum(starts[jnp.clip(group, 0, group_top)] - base, first)
        hi = jnp.minimum(ends[jnp.clip(group + tile_groups - 1, 0, group_top)] - base, last)
        begin, count = chunks(lo, hi, KT)
        queries = qa[pl.ds(at, QT), :]

        def step(num, state):
            top, total = state
            for part in range(KT // SUB):
                here = pl.multiple_of(begin + num * KT + part * SUB, GROUP)
                scores = rows_by_rows(ka[pl.ds(here, SUB), :], queries).reshape(SUB // 8, 8, QT)
                new_top = jnp.maximum(top, jnp.max(scores, axis=0))
                terms = jnp.sum(jnp.exp(scores - new_top[None]), axis=0)
                total = total * jnp.exp(top - new_top) + terms
                top = new_top
            return top, total

        top, total = lax.fori_loop(
            0, count, step, (jnp.full((8, QT), LOWEST, F32), jnp.zeros((8, QT), F32))
        )
        highest = jnp.max(top, axis=0, keepdims=True)
        line = highest + jnp.log(jnp.sum(total * jnp.exp(top - highest), axis=0, keepdims=True))
        line = jnp.where(highest < -0.5 * FAR, 0.0, line)
        for part in range(tile_groups):
            lse[pl.ds(tile * tile_groups + part, 1), :] = line[:, part * LANES : (part + 1) * LANES]
        return carry

    lax.fori_loop(first // QT, (last + QT - 1) // QT, totals, 0)

    tile_blocks = TILE // ROWS

    def own_columns(source, tile):
        columns = []
        for pair in range(tile_blocks // 2):
            group = BOARD_GROUPS + tile * tile_blocks + 2 * pair
            a, b = source[pl.ds(group, 1), :], source[pl.ds(group + 1, 1), :]
            line = jnp.where(
                low_row, jnp.where(swap, half_turn(a), a), jnp.where(swap, b, half_turn(b))
            )
            columns.append(jnp.transpose(jnp.broadcast_to(line, (GROUP, LANES))))
        return jnp.concatenate(columns, axis=0)

    def own_range(tile):
        group = outer * BOARD_GROUPS + tile * tile_blocks
        return chunks(starts[group] - base, ends[group + tile_blocks - 1] - base, KC)

    for tile in range(OWN // TILE):
        rows = slice(tile * TILE, (tile + 1) * TILE)
        begin, count = own_range(tile)
        logs = jnp.concatenate([own_columns(lse, tile)] * (KC // LANES), axis=1)
        drops = jnp.concatenate([own_columns(delta, tile)] * (KC // LANES), axis=1)
        acc[...] = jnp.zeros_like(acc)

        def step(num, carry):
            at = pl.multiple_of(begin + num * KC, GROUP)
            here = pl.ds(at, KC)
            weights = jnp.exp(rows_by_rows(own_qa[rows, :], ka[here, :]) - logs)
            grads = weights * (rows_by_rows(own_y[rows, :], xv[here, :]) - drops)
            acc[0] += rows_by_cols(grads.astype(BF16), ys[here, :])
            lines = [(begin + num * KC) // GROUP + part for part in range(KC // LANES)]
            logs_row = jnp.concatenate([lse[pl.ds(n, 1), :] for n in lines], axis=1)
            drops_row = jnp.concatenate([delta[pl.ds(n, 1), :] for n in lines], axis=1)
            weights = jnp.exp(rows_by_rows(own_ka[rows, :], qa[here, :]) - logs_row)
            grads = weights * (rows_by_rows(own_xv[rows, :], ys[here, :]) - drops_row)
            acc[1] += rows_by_cols(grads.astype(BF16), xs[here, :])
            acc[2] += rows_by_cols(weights.astype(BF16), ys[here, :])
            return carry

        lax.fori_loop(0, count, step, 0)
        dq = acc[0] * (1.0 / math.sqrt(HD))
        both = jnp.where(low_lanes(TILE), acc[1] * (1.0 / math.sqrt(HD)), acc[2]).astype(BF16)
        low_half = low_lanes(ROWS // 2)
        for block in range(tile_blocks):
            upper = dq[block * ROWS : block * ROWS + ROWS // 2]
            lower = dq[block * ROWS + ROWS // 2 : (block + 1) * ROWS]
            out_ref[tile * tile_blocks + block, ROWS:] = jnp.where(
                low_half, upper, half_turn(lower)
            ).astype(BF16)
            out_ref[tile * tile_blocks + block, :ROWS] = both[block * ROWS : (block + 1) * ROWS]


def main(meta, starts, ends, ids, pieces):
    smem = pl.BlockSpec(memory_space=pltpu.SMEM)
    vmem = pl.BlockSpec(memory_space=pltpu.VMEM)
    window = pltpu.VMEM((WINDOW + PAD, LANES), BF16)
    own = pltpu.VMEM((OWN, LANES), BF16)
    lines = pltpu.VMEM((GROUPS + 8 * (PAD // GROUP // 8 + 1), LANES), F32)
    return pl.pallas_call(
        main_kernel,
        out_shape=jax.ShapeDtypeStruct((BLOCKS, OUT_ROWS, LANES), BF16),
        in_specs=[smem, smem, smem, vmem] + [vmem] * 6,
        out_specs=vmem,
        scratch_shapes=[window] * 5 + [own] * 4 + [lines] * 2
        + [pltpu.VMEM((3, TILE, LANES), F32)],
        compiler_params=pltpu.CompilerParams(vmem_limit_bytes=32 * 1024 * 1024),
    )(meta, starts, ends, ids, *pieces)


def from_partner(x):
    return lax.ppermute(x, "head", [(h, 1 - h) for h in range(lax.axis_size("head"))])


def from_chip(x):
    return lax.ppermute(x, "outer", [(i, i ^ 1) for i in range(lax.axis_size("outer"))])


def from_next(x):
    heads, outers = lax.axis_size("head"), lax.axis_size("outer")
    pairs = []
    for h in range(heads):
        for i in range(1, outers - 1):
            to = i + 1 if i % 2 else i - 1
            pairs.append((h * outers + i, (1 - h) * outers + to))
    return lax.ppermute(x, ("head", "outer"), pairs)


def local(queries, keys, values, grad_out, saved_out, segment_ids):
    ids = segment_ids.reshape(-1, GROUP)
    starts = jnp.sum(segment_ids[None, :] < ids[:, :1], axis=1, dtype=jnp.int32)
    ends = jnp.sum(segment_ids[None, :] <= ids[:, -1:], axis=1, dtype=jnp.int32)
    meta = jnp.stack([lax.axis_index("outer"), lax.axis_index("inner"), lax.axis_index("head")])
    message = pack(queries, keys, values, grad_out, saved_out)
    mine = lax.all_to_all(message, "inner", split_axis=0, concat_axis=0, tiled=True)
    theirs = from_partner(mine)
    pieces = (
        mine,
        theirs,
        from_chip(mine),
        from_chip(theirs),
        from_next(mine),
        from_next(theirs),
    )
    results = main(meta, starts, ends, ids, pieces)
    gathered = lax.all_to_all(results, "inner", split_axis=0, concat_axis=0, tiled=True)
    return unpack(gathered)


def solution(mesh):
    rows = P(("outer", "inner", "head"), None)
    return jax.shard_map(
        local,
        mesh=mesh,
        in_specs=(rows, rows, rows, rows, rows, P()),
        out_specs=(rows, rows, rows),
        check_vma=False,
    )
```

```python
import math

import jax
import jax.numpy as jnp
from jax import lax
from jax.experimental import pallas as pl
from jax.experimental.pallas import tpu as pltpu
from jax.sharding import PartitionSpec as P

HD = 64
ROWS = 64
LANES = 128
BLOCKS = 8
MSG = 2 * ROWS + 16
OUT_ROWS = ROWS + ROWS // 2
BOARD = 1024
GROUP = 128
BOARD_GROUPS = BOARD // GROUP
WINDOW = 3 * BOARD
GROUPS = WINDOW // GROUP
OWN = BLOCKS * ROWS
QT = 512
KT = 1280
SUB = 128
KC = 768
TILE = 256
PAD = max(KC, KT)
FAR = 2.0**100
NO_LABEL = 63
BITS = 6
LOWEST = -3e38
F32 = jnp.float32
BF16 = jnp.bfloat16


def rows_by_rows(left, right):
    return lax.dot_general(left, right, (((1,), (1,)), ((), ())), preferred_element_type=F32)


def rows_by_cols(left, right):
    return lax.dot_general(left, right, (((1,), (0,)), ((), ())), preferred_element_type=F32)


def half_turn(x):
    return pltpu.roll(x, HD, axis=1)


def low_lanes(rows):
    return lax.broadcasted_iota(jnp.int32, (rows, LANES), 1) < HD


def pack_kernel(q_ref, k_ref, v_ref, g_ref, s_ref, out_ref):
    low = low_lanes(ROWS)
    for pair in range(4):
        cols = slice(pair * LANES, (pair + 1) * LANES)
        q, k, v, g = (r[:, cols].astype(F32) for r in (q_ref, k_ref, v_ref, g_ref))
        out_ref[2 * pair, :ROWS] = jnp.where(low, q, half_turn(v)).astype(BF16)
        out_ref[2 * pair + 1, :ROWS] = jnp.where(low, half_turn(q), v).astype(BF16)
        out_ref[2 * pair, ROWS : 2 * ROWS] = jnp.where(low, k, half_turn(g)).astype(BF16)
        out_ref[2 * pair + 1, ROWS : 2 * ROWS] = jnp.where(low, half_turn(k), g).astype(BF16)
    cols = 8 * HD
    products = g_ref[...].astype(F32) * s_ref[...].astype(F32)
    high = products.astype(BF16)
    rest = (products - high.astype(F32)).astype(BF16)
    head_of = lax.broadcasted_iota(jnp.int32, (16, cols), 1) // HD
    wanted = lax.broadcasted_iota(jnp.int32, (16, cols), 0) % 8
    pick = jnp.where(head_of == wanted, 1.0, 0.0).astype(BF16)
    twice = lambda x: jnp.concatenate([x, x], axis=0)
    deltas = rows_by_rows(pick, twice(high)) + rows_by_rows(pick, twice(rest))
    first = deltas.astype(BF16).astype(F32)
    second = (deltas - first).astype(BF16).astype(F32)
    third = deltas - first - second
    row = lax.broadcasted_iota(jnp.int32, (16, LANES), 0)
    lowest = low_lanes(16)
    table = jnp.where(
        row < 8, jnp.where(lowest, first, second), jnp.where(lowest, third, 0.0)
    ).astype(BF16)
    for head in range(8):
        out_ref[head, 2 * ROWS :] = table


def pack(queries, keys, values, grad_out, saved_out):
    return pl.pallas_call(
        pack_kernel,
        out_shape=jax.ShapeDtypeStruct((8, MSG, LANES), BF16),
    )(queries, keys, values, grad_out, saved_out)


def unpack_kernel(in_ref, dq_ref, dk_ref, dv_ref):
    low = low_lanes(ROWS)
    low_half = low_lanes(ROWS // 2)
    for pair in range(4):
        cols = slice(pair * LANES, (pair + 1) * LANES)
        a = in_ref[2 * pair, :ROWS].astype(F32)
        b = in_ref[2 * pair + 1, :ROWS].astype(F32)
        dk_ref[:, cols] = jnp.where(low, a, half_turn(b)).astype(BF16)
        dv_ref[:, cols] = jnp.where(low, half_turn(a), b).astype(BF16)
        c = in_ref[2 * pair, ROWS:].astype(F32)
        d = in_ref[2 * pair + 1, ROWS:].astype(F32)
        dq_ref[: ROWS // 2, cols] = jnp.where(low_half, c, half_turn(d)).astype(BF16)
        dq_ref[ROWS // 2 :, cols] = jnp.where(low_half, half_turn(c), d).astype(BF16)


def unpack(results):
    shape = jax.ShapeDtypeStruct((ROWS, 8 * HD), BF16)
    return pl.pallas_call(unpack_kernel, out_shape=(shape, shape, shape))(results)


def features(ids, lane, lead):
    at = lane - lead
    second = at >= BITS
    bit = lax.shift_right_logical(ids, jnp.where(second, at - BITS, at) & 31) & 1
    used = jnp.logical_and(at >= 0, at < 2 * BITS)
    return used, jnp.where(second, 1 - bit, bit).astype(F32)


def main_kernel(
    meta, starts, ends, ids_ref, p0, p1, p2, p3, p4, p5, out_ref,
    xs, ys, qa, ka, xv, own_qa, own_ka, own_xv, own_y, lse, delta, acc,
):
    outer, head, parity = meta[0], meta[1], meta[2]
    base = (outer - 1) * BOARD
    lane = lax.broadcasted_iota(jnp.int32, (GROUP, LANES), 1)
    low = lane < HD
    low_row = low_lanes(1)
    sub16 = lax.broadcasted_iota(jnp.int32, (16, LANES), 0)
    delta_rows = jnp.logical_or(sub16 == head, sub16 == head + 8)

    swap = parity == 1
    odd = outer % 2
    placed = (
        (1, p0, p1, parity),
        (2 - 2 * odd, p2, p3, parity),
        (2 * odd, p4, p5, 1 - parity),
    )
    for board, mine, other, mine_side in placed:
        for block in range(BLOCKS):
            group = board * BLOCKS + block
            for piece, side in ((mine, mine_side), (other, 1 - mine_side)):
                at = pl.multiple_of(group * GROUP + side * ROWS, ROWS)
                xs[pl.ds(at, ROWS), :] = piece[block, :ROWS]
                ys[pl.ds(at, ROWS), :] = piece[block, ROWS : 2 * ROWS]
            parts = []
            for piece in (mine, other):
                table = jnp.where(delta_rows, piece[block, 2 * ROWS :].astype(F32), 0.0)
                line = jnp.sum(table, axis=0, keepdims=True)
                parts.append(line + half_turn(line))
            delta[pl.ds(group, 1), :] = jnp.where(
                jnp.logical_xor(low_row, mine_side == 1), parts[0], parts[1]
            )

    def prepare(group, carry):
        at = pl.multiple_of(group * GROUP, GROUP)
        board = outer - 1 + group // BOARD_GROUPS
        real = jnp.logical_and(board >= 0, board < ids_ref.shape[0] // BOARD_GROUPS)
        line = ids_ref[pl.ds(jnp.clip(base // GROUP + group, 0, ids_ref.shape[0] - 1), 1), :]
        line = jnp.where(real, line, NO_LABEL)
        ids = jnp.transpose(jnp.broadcast_to(line, (GROUP, LANES)))
        used, bits = features(ids, lane, HD)
        x = xs[pl.ds(at, GROUP), :].astype(F32)
        y = ys[pl.ds(at, GROUP), :].astype(F32)
        q_side = jnp.where(used, -FAR * bits, 0.0)
        k_side = jnp.where(used, 1.0 - bits, 0.0)
        qa[pl.ds(at, GROUP), :] = jnp.where(low, x * (1.0 / math.sqrt(HD)), q_side).astype(BF16)
        ka[pl.ds(at, GROUP), :] = jnp.where(low, y, k_side).astype(BF16)
        xv[pl.ds(at, GROUP), :] = jnp.where(low, 0.0, x).astype(BF16)
        return carry

    lax.fori_loop(0, GROUPS, prepare, 0, unroll=12)
    _, bits = features(jnp.full((PAD, LANES), NO_LABEL, jnp.int32),
                       lax.broadcasted_iota(jnp.int32, (PAD, LANES), 1), HD)
    pad_lane = lax.broadcasted_iota(jnp.int32, (PAD, LANES), 1)
    pad_used = jnp.logical_and(pad_lane >= HD, pad_lane < HD + 2 * BITS)
    zero = jnp.zeros((PAD, LANES), BF16)
    qa[WINDOW:, :] = jnp.where(pad_used, -FAR * bits, 0.0).astype(BF16)
    ka[WINDOW:, :] = jnp.where(pad_used, 1.0 - bits, 0.0).astype(BF16)
    xv[WINDOW:, :] = zero
    xs[WINDOW:, :] = zero
    ys[WINDOW:, :] = zero
    lse[...] = jnp.zeros_like(lse)
    delta[pl.ds(GROUPS, delta.shape[0] - GROUPS), :] = jnp.zeros(
        (delta.shape[0] - GROUPS, LANES), F32
    )

    for block in range(BLOCKS):
        at = pl.multiple_of(BOARD + block * GROUP + parity * ROWS, ROWS)
        to = pl.ds(block * ROWS, ROWS)
        own_qa[to, :] = qa[pl.ds(at, ROWS), :]
        own_ka[to, :] = ka[pl.ds(at, ROWS), :]
        own_xv[to, :] = xv[pl.ds(at, ROWS), :]
        own_y[to, :] = ys[pl.ds(at, ROWS), :]

    first = starts[outer * BOARD_GROUPS] - base
    last = ends[outer * BOARD_GROUPS + BOARD_GROUPS - 1] - base
    tile_groups = QT // GROUP

    def chunks(lo, hi, size):
        begin = lo // GROUP * GROUP
        return begin, (hi - begin + size - 1) // size

    def totals(tile, carry):
        at = pl.multiple_of(tile * QT, QT)
        group = outer * BOARD_GROUPS - BOARD_GROUPS + tile * tile_groups
        group_top = starts.shape[0] - 1
        lo = jnp.maximum(starts[jnp.clip(group, 0, group_top)] - base, first)
        hi = jnp.minimum(ends[jnp.clip(group + tile_groups - 1, 0, group_top)] - base, last)
        begin, count = chunks(lo, hi, KT)
        queries = qa[pl.ds(at, QT), :]

        def step(num, state):
            top, total = state
            for part in range(KT // SUB):
                here = pl.multiple_of(begin + num * KT + part * SUB, GROUP)
                scores = rows_by_rows(ka[pl.ds(here, SUB), :], queries).reshape(SUB // 8, 8, QT)
                new_top = jnp.maximum(top, jnp.max(scores, axis=0))
                terms = jnp.sum(jnp.exp(scores - new_top[None]), axis=0)
                total = total * jnp.exp(top - new_top) + terms
                top = new_top
            return top, total

        top, total = lax.fori_loop(
            0, count, step, (jnp.full((8, QT), LOWEST, F32), jnp.zeros((8, QT), F32))
        )
        highest = jnp.max(top, axis=0, keepdims=True)
        line = highest + jnp.log(jnp.sum(total * jnp.exp(top - highest), axis=0, keepdims=True))
        line = jnp.where(highest < -0.5 * FAR, 0.0, line)
        for part in range(tile_groups):
            lse[pl.ds(tile * tile_groups + part, 1), :] = line[:, part * LANES : (part + 1) * LANES]
        return carry

    lax.fori_loop(first // QT, (last + QT - 1) // QT, totals, 0)

    tile_blocks = TILE // ROWS

    def own_columns(source, tile):
        columns = []
        for pair in range(tile_blocks // 2):
            group = BOARD_GROUPS + tile * tile_blocks + 2 * pair
            a, b = source[pl.ds(group, 1), :], source[pl.ds(group + 1, 1), :]
            line = jnp.where(
                low_row, jnp.where(swap, half_turn(a), a), jnp.where(swap, b, half_turn(b))
            )
            columns.append(jnp.transpose(jnp.broadcast_to(line, (GROUP, LANES))))
        return jnp.concatenate(columns, axis=0)

    def own_range(tile):
        group = outer * BOARD_GROUPS + tile * tile_blocks
        return chunks(starts[group] - base, ends[group + tile_blocks - 1] - base, KC)

    for tile in range(OWN // TILE):
        rows = slice(tile * TILE, (tile + 1) * TILE)
        begin, count = own_range(tile)
        logs = jnp.concatenate([own_columns(lse, tile)] * (KC // LANES), axis=1)
        drops = jnp.concatenate([own_columns(delta, tile)] * (KC // LANES), axis=1)
        acc[...] = jnp.zeros_like(acc)

        def step(num, carry):
            at = pl.multiple_of(begin + num * KC, GROUP)
            here = pl.ds(at, KC)
            weights = jnp.exp(rows_by_rows(own_qa[rows, :], ka[here, :]) - logs)
            grads = weights * (rows_by_rows(own_y[rows, :], xv[here, :]) - drops)
            acc[0] += rows_by_cols(grads.astype(BF16), ys[here, :])
            lines = [(begin + num * KC) // GROUP + part for part in range(KC // LANES)]
            logs_row = jnp.concatenate([lse[pl.ds(n, 1), :] for n in lines], axis=1)
            drops_row = jnp.concatenate([delta[pl.ds(n, 1), :] for n in lines], axis=1)
            weights = jnp.exp(rows_by_rows(own_ka[rows, :], qa[here, :]) - logs_row)
            grads = weights * (rows_by_rows(own_xv[rows, :], ys[here, :]) - drops_row)
            acc[1] += rows_by_cols(grads.astype(BF16), xs[here, :])
            acc[2] += rows_by_cols(weights.astype(BF16), ys[here, :])
            return carry

        lax.fori_loop(0, count, step, 0)
        dq = acc[0] * (1.0 / math.sqrt(HD))
        both = jnp.where(low_lanes(TILE), acc[1] * (1.0 / math.sqrt(HD)), acc[2]).astype(BF16)
        low_half = low_lanes(ROWS // 2)
        for block in range(tile_blocks):
            upper = dq[block * ROWS : block * ROWS + ROWS // 2]
            lower = dq[block * ROWS + ROWS // 2 : (block + 1) * ROWS]
            out_ref[tile * tile_blocks + block, ROWS:] = jnp.where(
                low_half, upper, half_turn(lower)
            ).astype(BF16)
            out_ref[tile * tile_blocks + block, :ROWS] = both[block * ROWS : (block + 1) * ROWS]


def main(meta, starts, ends, ids, pieces):
    smem = pl.BlockSpec(memory_space=pltpu.SMEM)
    vmem = pl.BlockSpec(memory_space=pltpu.VMEM)
    window = pltpu.VMEM((WINDOW + PAD, LANES), BF16)
    own = pltpu.VMEM((OWN, LANES), BF16)
    lines = pltpu.VMEM((GROUPS + 8 * (PAD // GROUP // 8 + 1), LANES), F32)
    return pl.pallas_call(
        main_kernel,
        out_shape=jax.ShapeDtypeStruct((BLOCKS, OUT_ROWS, LANES), BF16),
        in_specs=[smem, smem, smem, vmem] + [vmem] * 6,
        out_specs=vmem,
        scratch_shapes=[window] * 5 + [own] * 4 + [lines] * 2
        + [pltpu.VMEM((3, TILE, LANES), F32)],
        compiler_params=pltpu.CompilerParams(vmem_limit_bytes=32 * 1024 * 1024),
    )(meta, starts, ends, ids, *pieces)


def from_partner(x):
    return lax.ppermute(x, "head", [(h, 1 - h) for h in range(lax.axis_size("head"))])


def from_chip(x):
    return lax.ppermute(x, "outer", [(i, i ^ 1) for i in range(lax.axis_size("outer"))])


def from_next(x):
    heads, outers = lax.axis_size("head"), lax.axis_size("outer")
    pairs = []
    for h in range(heads):
        for i in range(1, outers - 1):
            to = i + 1 if i % 2 else i - 1
            pairs.append((h * outers + i, (1 - h) * outers + to))
    return lax.ppermute(x, ("head", "outer"), pairs)


def local(queries, keys, values, grad_out, saved_out, segment_ids):
    ids = segment_ids.reshape(-1, GROUP)
    starts = jnp.sum(segment_ids[None, :] < ids[:, :1], axis=1, dtype=jnp.int32)
    ends = jnp.sum(segment_ids[None, :] <= ids[:, -1:], axis=1, dtype=jnp.int32)
    meta = jnp.stack([lax.axis_index("outer"), lax.axis_index("inner"), lax.axis_index("head")])
    message = pack(queries, keys, values, grad_out, saved_out)
    mine = lax.all_to_all(message, "inner", split_axis=0, concat_axis=0, tiled=True)
    next_mine = from_next(mine)
    theirs = from_partner(mine)
    next_theirs = from_next(theirs)
    pieces = (mine, theirs, from_chip(mine), from_chip(theirs), next_mine, next_theirs)
    results = main(meta, starts, ends, ids, pieces)
    gathered = lax.all_to_all(results, "inner", split_axis=0, concat_axis=0, tiled=True)
    return unpack(gathered)


def solution(mesh):
    rows = P(("outer", "inner", "head"), None)
    return jax.shard_map(
        local,
        mesh=mesh,
        in_specs=(rows, rows, rows, rows, rows, P()),
        out_specs=(rows, rows, rows),
        check_vma=False,
    )
```

```python
import math

import jax
import jax.numpy as jnp
from jax import lax
from jax.experimental import pallas as pl
from jax.experimental.pallas import tpu as pltpu
from jax.sharding import PartitionSpec as P

HD = 64
ROWS = 64
LANES = 128
BLOCKS = 8
MSG = 2 * ROWS + 16
OUT_ROWS = ROWS + ROWS // 2
BOARD = 1024
GROUP = 128
BOARD_GROUPS = BOARD // GROUP
WINDOW = 3 * BOARD
GROUPS = WINDOW // GROUP
OWN = BLOCKS * ROWS
QT = 512
KT = 640
SUB = 128
KC = 768
TILE = 256
PAD = max(KC, KT)
FAR = 2.0**100
NO_LABEL = 63
LABELS = 32
BITS = 6
LOWEST = -3e38
F32 = jnp.float32
BF16 = jnp.bfloat16


def rows_by_rows(left, right):
    return lax.dot_general(left, right, (((1,), (1,)), ((), ())), preferred_element_type=F32)


def rows_by_cols(left, right):
    return lax.dot_general(left, right, (((1,), (0,)), ((), ())), preferred_element_type=F32)


def half_turn(x):
    return pltpu.roll(x, HD, axis=1)


def low_lanes(rows):
    return lax.broadcasted_iota(jnp.int32, (rows, LANES), 1) < HD


def pack_kernel(q_ref, k_ref, v_ref, g_ref, s_ref, out_ref):
    low = low_lanes(ROWS)
    for pair in range(4):
        cols = slice(pair * LANES, (pair + 1) * LANES)
        q, k, v, g = (r[:, cols].astype(F32) for r in (q_ref, k_ref, v_ref, g_ref))
        out_ref[2 * pair, :ROWS] = jnp.where(low, q, half_turn(v)).astype(BF16)
        out_ref[2 * pair + 1, :ROWS] = jnp.where(low, half_turn(q), v).astype(BF16)
        out_ref[2 * pair, ROWS : 2 * ROWS] = jnp.where(low, k, half_turn(g)).astype(BF16)
        out_ref[2 * pair + 1, ROWS : 2 * ROWS] = jnp.where(low, half_turn(k), g).astype(BF16)
    cols = 8 * HD
    products = g_ref[...].astype(F32) * s_ref[...].astype(F32)
    high = products.astype(BF16)
    rest = (products - high.astype(F32)).astype(BF16)
    head_of = lax.broadcasted_iota(jnp.int32, (16, cols), 1) // HD
    wanted = lax.broadcasted_iota(jnp.int32, (16, cols), 0) % 8
    pick = jnp.where(head_of == wanted, 1.0, 0.0).astype(BF16)
    twice = lambda x: jnp.concatenate([x, x], axis=0)
    deltas = rows_by_rows(pick, twice(high)) + rows_by_rows(pick, twice(rest))
    first = deltas.astype(BF16).astype(F32)
    second = (deltas - first).astype(BF16).astype(F32)
    third = deltas - first - second
    row = lax.broadcasted_iota(jnp.int32, (16, LANES), 0)
    lowest = low_lanes(16)
    table = jnp.where(
        row < 8, jnp.where(lowest, first, second), jnp.where(lowest, third, 0.0)
    ).astype(BF16)
    for head in range(8):
        out_ref[head, 2 * ROWS :] = table


def pack(queries, keys, values, grad_out, saved_out):
    return pl.pallas_call(
        pack_kernel,
        out_shape=jax.ShapeDtypeStruct((8, MSG, LANES), BF16),
    )(queries, keys, values, grad_out, saved_out)


def unpack_kernel(in_ref, dq_ref, dk_ref, dv_ref):
    low = low_lanes(ROWS)
    low_half = low_lanes(ROWS // 2)
    for pair in range(4):
        cols = slice(pair * LANES, (pair + 1) * LANES)
        a = in_ref[2 * pair, :ROWS].astype(F32)
        b = in_ref[2 * pair + 1, :ROWS].astype(F32)
        dk_ref[:, cols] = jnp.where(low, a, half_turn(b)).astype(BF16)
        dv_ref[:, cols] = jnp.where(low, half_turn(a), b).astype(BF16)
        c = in_ref[2 * pair, ROWS:].astype(F32)
        d = in_ref[2 * pair + 1, ROWS:].astype(F32)
        dq_ref[: ROWS // 2, cols] = jnp.where(low_half, c, half_turn(d)).astype(BF16)
        dq_ref[ROWS // 2 :, cols] = jnp.where(low_half, half_turn(c), d).astype(BF16)


def unpack(results):
    shape = jax.ShapeDtypeStruct((ROWS, 8 * HD), BF16)
    return pl.pallas_call(unpack_kernel, out_shape=(shape, shape, shape))(results)


def features(ids, lane, lead):
    at = lane - lead
    second = at >= BITS
    bit = lax.shift_right_logical(ids, jnp.where(second, at - BITS, at) & 31) & 1
    used = jnp.logical_and(at >= 0, at < 2 * BITS)
    return used, jnp.where(second, 1 - bit, bit).astype(F32)


def main_kernel(
    meta, starts, ends, ids_ref, p0, p1, p2, p3, p4, p5, out_ref,
    xs, ys, qa, ka, xv, own_qa, own_ka, own_xv, own_y, lse, delta, acc,
):
    outer, head, parity = meta[0], meta[1], meta[2]
    base = (outer - 1) * BOARD
    lane = lax.broadcasted_iota(jnp.int32, (GROUP, LANES), 1)
    low = lane < HD
    low_row = low_lanes(1)
    sub16 = lax.broadcasted_iota(jnp.int32, (16, LANES), 0)
    delta_rows = jnp.logical_or(sub16 == head, sub16 == head + 8)

    swap = parity == 1
    odd = outer % 2
    placed = (
        (1, p0, p1, parity),
        (2 - 2 * odd, p2, p3, parity),
        (2 * odd, p4, p5, 1 - parity),
    )
    for board, mine, other, mine_side in placed:
        for block in range(BLOCKS):
            group = board * BLOCKS + block
            for piece, side in ((mine, mine_side), (other, 1 - mine_side)):
                at = pl.multiple_of(group * GROUP + side * ROWS, ROWS)
                xs[pl.ds(at, ROWS), :] = piece[block, :ROWS]
                ys[pl.ds(at, ROWS), :] = piece[block, ROWS : 2 * ROWS]
            parts = []
            for piece in (mine, other):
                table = jnp.where(delta_rows, piece[block, 2 * ROWS :].astype(F32), 0.0)
                line = jnp.sum(table, axis=0, keepdims=True)
                parts.append(line + half_turn(line))
            delta[pl.ds(group, 1), :] = jnp.where(
                jnp.logical_xor(low_row, mine_side == 1), parts[0], parts[1]
            )

    def prepare(group, carry):
        at = pl.multiple_of(group * GROUP, GROUP)
        board = outer - 1 + group // BOARD_GROUPS
        real = jnp.logical_and(board >= 0, board < ids_ref.shape[0] // BOARD_GROUPS)
        line = ids_ref[pl.ds(jnp.clip(base // GROUP + group, 0, ids_ref.shape[0] - 1), 1), :]
        line = jnp.where(real, line, NO_LABEL)
        ids = jnp.transpose(jnp.broadcast_to(line, (GROUP, LANES)))
        used, bits = features(ids, lane, HD)
        x = xs[pl.ds(at, GROUP), :].astype(F32)
        y = ys[pl.ds(at, GROUP), :].astype(F32)
        q_side = jnp.where(used, -FAR * bits, 0.0)
        k_side = jnp.where(used, 1.0 - bits, 0.0)
        qa[pl.ds(at, GROUP), :] = jnp.where(low, x * (1.0 / math.sqrt(HD)), q_side).astype(BF16)
        ka[pl.ds(at, GROUP), :] = jnp.where(low, y, k_side).astype(BF16)
        xv[pl.ds(at, GROUP), :] = jnp.where(low, 0.0, x).astype(BF16)
        return carry

    lax.fori_loop(0, GROUPS, prepare, 0, unroll=12)
    _, bits = features(jnp.full((PAD, LANES), NO_LABEL, jnp.int32),
                       lax.broadcasted_iota(jnp.int32, (PAD, LANES), 1), HD)
    pad_lane = lax.broadcasted_iota(jnp.int32, (PAD, LANES), 1)
    pad_used = jnp.logical_and(pad_lane >= HD, pad_lane < HD + 2 * BITS)
    zero = jnp.zeros((PAD, LANES), BF16)
    qa[WINDOW:, :] = jnp.where(pad_used, -FAR * bits, 0.0).astype(BF16)
    ka[WINDOW:, :] = jnp.where(pad_used, 1.0 - bits, 0.0).astype(BF16)
    xv[WINDOW:, :] = zero
    xs[WINDOW:, :] = zero
    ys[WINDOW:, :] = zero
    lse[...] = jnp.zeros_like(lse)
    delta[pl.ds(GROUPS, delta.shape[0] - GROUPS), :] = jnp.zeros(
        (delta.shape[0] - GROUPS, LANES), F32
    )

    for block in range(BLOCKS):
        at = pl.multiple_of(BOARD + block * GROUP + parity * ROWS, ROWS)
        to = pl.ds(block * ROWS, ROWS)
        own_qa[to, :] = qa[pl.ds(at, ROWS), :]
        own_ka[to, :] = ka[pl.ds(at, ROWS), :]
        own_xv[to, :] = xv[pl.ds(at, ROWS), :]
        own_y[to, :] = ys[pl.ds(at, ROWS), :]

    first = starts[outer * BOARD_GROUPS] - base
    last = ends[outer * BOARD_GROUPS + BOARD_GROUPS - 1] - base
    tile_groups = QT // GROUP

    def chunks(lo, hi, size):
        begin = lo // GROUP * GROUP
        return begin, (hi - begin + size - 1) // size

    def totals(tile, carry):
        at = pl.multiple_of(tile * QT, QT)
        group = outer * BOARD_GROUPS - BOARD_GROUPS + tile * tile_groups
        group_top = starts.shape[0] - 1
        lo = jnp.maximum(starts[jnp.clip(group, 0, group_top)] - base, first)
        hi = jnp.minimum(ends[jnp.clip(group + tile_groups - 1, 0, group_top)] - base, last)
        begin, count = chunks(lo, hi, KT)
        queries = qa[pl.ds(at, QT), :]

        def step(num, state):
            top, total = state
            for part in range(KT // SUB):
                here = pl.multiple_of(begin + num * KT + part * SUB, GROUP)
                scores = rows_by_rows(ka[pl.ds(here, SUB), :], queries).reshape(SUB // 8, 8, QT)
                new_top = jnp.maximum(top, jnp.max(scores, axis=0))
                terms = jnp.sum(jnp.exp(scores - new_top[None]), axis=0)
                total = total * jnp.exp(top - new_top) + terms
                top = new_top
            return top, total

        top, total = lax.fori_loop(
            0, count, step, (jnp.full((8, QT), LOWEST, F32), jnp.zeros((8, QT), F32))
        )
        highest = jnp.max(top, axis=0, keepdims=True)
        line = highest + jnp.log(jnp.sum(total * jnp.exp(top - highest), axis=0, keepdims=True))
        line = jnp.where(highest < -0.5 * FAR, 0.0, line)
        for part in range(tile_groups):
            lse[pl.ds(tile * tile_groups + part, 1), :] = line[:, part * LANES : (part + 1) * LANES]
        return carry

    lax.fori_loop(first // QT, (last + QT - 1) // QT, totals, 0)

    tile_blocks = TILE // ROWS

    def own_columns(source, tile):
        columns = []
        for pair in range(tile_blocks // 2):
            group = BOARD_GROUPS + tile * tile_blocks + 2 * pair
            a, b = source[pl.ds(group, 1), :], source[pl.ds(group + 1, 1), :]
            line = jnp.where(
                low_row, jnp.where(swap, half_turn(a), a), jnp.where(swap, b, half_turn(b))
            )
            columns.append(jnp.transpose(jnp.broadcast_to(line, (GROUP, LANES))))
        return jnp.concatenate(columns, axis=0)

    def own_range(tile):
        group = outer * BOARD_GROUPS + tile * tile_blocks
        return chunks(starts[group] - base, ends[group + tile_blocks - 1] - base, KC)

    for tile in range(OWN // TILE):
        rows = slice(tile * TILE, (tile + 1) * TILE)
        begin, count = own_range(tile)
        logs = jnp.concatenate([own_columns(lse, tile)] * (KC // LANES), axis=1)
        drops = jnp.concatenate([own_columns(delta, tile)] * (KC // LANES), axis=1)
        acc[...] = jnp.zeros_like(acc)

        def step(num, carry):
            at = pl.multiple_of(begin + num * KC, GROUP)
            here = pl.ds(at, KC)
            weights = jnp.exp(rows_by_rows(own_qa[rows, :], ka[here, :]) - logs)
            grads = weights * (rows_by_rows(own_y[rows, :], xv[here, :]) - drops)
            acc[0] += rows_by_cols(grads.astype(BF16), ys[here, :])
            lines = [(begin + num * KC) // GROUP + part for part in range(KC // LANES)]
            logs_row = jnp.concatenate([lse[pl.ds(n, 1), :] for n in lines], axis=1)
            drops_row = jnp.concatenate([delta[pl.ds(n, 1), :] for n in lines], axis=1)
            weights = jnp.exp(rows_by_rows(own_ka[rows, :], qa[here, :]) - logs_row)
            grads = weights * (rows_by_rows(own_xv[rows, :], ys[here, :]) - drops_row)
            acc[1] += rows_by_cols(grads.astype(BF16), xs[here, :])
            acc[2] += rows_by_cols(weights.astype(BF16), ys[here, :])
            return carry

        lax.fori_loop(0, count, step, 0)
        dq = acc[0] * (1.0 / math.sqrt(HD))
        both = jnp.where(low_lanes(TILE), acc[1] * (1.0 / math.sqrt(HD)), acc[2]).astype(BF16)
        low_half = low_lanes(ROWS // 2)
        for block in range(tile_blocks):
            upper = dq[block * ROWS : block * ROWS + ROWS // 2]
            lower = dq[block * ROWS + ROWS // 2 : (block + 1) * ROWS]
            out_ref[tile * tile_blocks + block, ROWS:] = jnp.where(
                low_half, upper, half_turn(lower)
            ).astype(BF16)
            out_ref[tile * tile_blocks + block, :ROWS] = both[block * ROWS : (block + 1) * ROWS]


def main(meta, starts, ends, ids, pieces):
    smem = pl.BlockSpec(memory_space=pltpu.SMEM)
    vmem = pl.BlockSpec(memory_space=pltpu.VMEM)
    window = pltpu.VMEM((WINDOW + PAD, LANES), BF16)
    own = pltpu.VMEM((OWN, LANES), BF16)
    lines = pltpu.VMEM((GROUPS + 8 * (PAD // GROUP // 8 + 1), LANES), F32)
    return pl.pallas_call(
        main_kernel,
        out_shape=jax.ShapeDtypeStruct((BLOCKS, OUT_ROWS, LANES), BF16),
        in_specs=[smem, smem, smem, vmem] + [vmem] * 6,
        out_specs=vmem,
        scratch_shapes=[window] * 5 + [own] * 4 + [lines] * 2
        + [pltpu.VMEM((3, TILE, LANES), F32)],
        compiler_params=pltpu.CompilerParams(vmem_limit_bytes=32 * 1024 * 1024),
    )(meta, starts, ends, ids, *pieces)


def from_partner(x):
    return lax.ppermute(x, "head", [(h, 1 - h) for h in range(lax.axis_size("head"))])


def from_chip(x):
    return lax.ppermute(x, "outer", [(i, i ^ 1) for i in range(lax.axis_size("outer"))])


def from_next(x):
    heads, outers = lax.axis_size("head"), lax.axis_size("outer")
    pairs = []
    for h in range(heads):
        for i in range(1, outers - 1):
            to = i + 1 if i % 2 else i - 1
            pairs.append((h * outers + i, (1 - h) * outers + to))
    return lax.ppermute(x, ("head", "outer"), pairs)


def local(queries, keys, values, grad_out, saved_out, segment_ids):
    ids = segment_ids.reshape(-1, GROUP)
    labels = jnp.arange(LABELS, dtype=jnp.int32)
    before = jnp.sum(segment_ids[None, :] < labels[:, None], axis=1, dtype=jnp.int32)
    through = jnp.sum(segment_ids[None, :] <= labels[:, None], axis=1, dtype=jnp.int32)
    starts = jnp.sum(jnp.where(ids[:, :1] == labels, before, 0), axis=1, dtype=jnp.int32)
    ends = jnp.sum(jnp.where(ids[:, -1:] == labels, through, 0), axis=1, dtype=jnp.int32)
    meta = jnp.stack([lax.axis_index("outer"), lax.axis_index("inner"), lax.axis_index("head")])
    message = pack(queries, keys, values, grad_out, saved_out)
    mine = lax.all_to_all(message, "inner", split_axis=0, concat_axis=0, tiled=True)
    theirs = from_partner(mine)
    pieces = (
        mine,
        theirs,
        from_chip(mine),
        from_chip(theirs),
        from_next(mine),
        from_next(theirs),
    )
    results = main(meta, starts, ends, ids, pieces)
    gathered = lax.all_to_all(results, "inner", split_axis=0, concat_axis=0, tiled=True)
    return unpack(gathered)


def solution(mesh):
    rows = P(("outer", "inner", "head"), None)
    return jax.shard_map(
        local,
        mesh=mesh,
        in_specs=(rows, rows, rows, rows, rows, P()),
        out_specs=(rows, rows, rows),
        check_vma=False,
    )
```
